32 devices in a mesh: dp: 8 (over y, x, core), tensor: 4 (over z).
Axes of the slice: x: 2, y: 2, z: 4, core: 2. Of those that a mesh axis runs over, the one named last changes fastest.
Arguments:
- tokens: bfloat16 [25216, 768], P('dp'), may hold values from -6 to 6
- cotangent: bfloat16 [25216, 768], P('dp'), may hold values from -6 to 6
- qkv_weight: float32 [3, 768, 768], P(None, 'dp', 'tensor'), may hold values from -0.21875 to 0.21875
- out_weight: float32 [768, 768], P('tensor', 'dp'), may hold values from -0.875 to 0.875
- up_weight: float32 [768, 3072], P('dp', 'tensor'), may hold values from -0.21875 to 0.21875
- down_weight: float32 [3072, 768], P('tensor', 'dp'), may hold values from -0.109375 to 0.109375
- shared_vectors: float32 [6, 768], P(None, 'dp'), may hold values from -0.5 to 1.4, as said below
- split_vectors: float32 [4, 1152], P('tensor', 'dp'), may hold values from -1.5 to 1.5
- qkv_first: float32 [3, 768, 768], P(None, 'dp', 'tensor'), may hold values from -80 to 80
- qkv_second: float32 [3, 768, 768], P(None, 'dp', 'tensor'), may hold values from 6.304 to 100.864
- out_first: float32 [768, 768], P('tensor', 'dp'), may hold values from -16 to 16
- out_second: float32 [768, 768], P('tensor', 'dp'), may hold values from 0.25216 to 4.03456
- up_first: float32 [768, 3072], P('dp', 'tensor'), may hold values from -32 to 32
- up_second: float32 [768, 3072], P('dp', 'tensor'), may hold values from 1.13472 to 18.15552
- down_first: float32 [3072, 768], P('tensor', 'dp'), may hold values from -64 to 64
- down_second: float32 [3072, 768], P('tensor', 'dp'), may hold values from 4.53888 to 73.1264
- shared_first: float32 [6, 768], P(None, 'dp'), may hold values from -80 to 80
- shared_second: float32 [6, 768], P(None, 'dp'), may hold values from 6.304 to 100.864
- split_first: float32 [4, 1152], P('tensor', 'dp'), may hold values from -80 to 80
- split_second: float32 [4, 1152], P('tensor', 'dp'), may hold values from 6.304 to 100.864
Outputs:
- block_out: bfloat16 [25216, 768], P('dp')
- tokens_grad: bfloat16 [25216, 768], P('dp')
- qkv_first_new: float32 [3, 768, 768], P(None, 'dp', 'tensor')
- qkv_second_new: float32 [3, 768, 768], P(None, 'dp', 'tensor')
- qkv_updated: float32 [3, 768, 768], P(None, 'dp', 'tensor')
- out_first_new: float32 [768, 768], P('tensor', 'dp')
- out_second_new: float32 [768, 768], P('tensor', 'dp')
- out_updated: float32 [768, 768], P('tensor', 'dp')
- up_first_new: float32 [768, 3072], P('dp', 'tensor')
- up_second_new: float32 [768, 3072], P('dp', 'tensor')
- up_updated: float32 [768, 3072], P('dp', 'tensor')
- down_first_new: float32 [3072, 768], P('tensor', 'dp')
- down_second_new: float32 [3072, 768], P('tensor', 'dp')
- down_updated: float32 [3072, 768], P('tensor', 'dp')
- shared_first_new: float32 [6, 768], P(None, 'dp')
- shared_second_new: float32 [6, 768], P(None, 'dp')
- shared_updated: float32 [6, 768], P(None, 'dp')
- split_first_new: float32 [4, 1152], P('tensor', 'dp')
- split_second_new: float32 [4, 1152], P('tensor', 'dp')
- split_updated: float32 [4, 1152], P('tensor', 'dp')
The draws below stay inside these ranges and needn't reach their ends.
Inputs may be any that keep to these rules, and one draw needn't show every extreme that they name: `shared_vectors`: rows 0 and 2 lie in 0.6 to 1.4, the other rows in -0.5 to 0.5.
All inputs are finite; a program needn't handle non-finite values.
Results may differ from the reference program's by a relative error of at most 0.025.
Values may be sent and summed in bfloat16 or wider, within the bound.
A program may use at most 192 MiB of HBM per device.

```python
import math
import jax
import jax.numpy as jnp
from jax import lax

D = 768
HEADS = 12
HEAD = 64
FF = 3072
SEQ = 197
IMG_DEV = 16
STEP = 10
TOKENS = 25216
N_DP = 8
N_TENSOR = 4


def draw_shared_vectors(key, part):
    key = jax.random.fold_in(key, 11)
    gain_key, shift_key = jax.random.split(key)
    gains = jax.random.uniform(gain_key, (2, D), jnp.float32, 0.6, 1.4)
    shifts = jax.random.uniform(shift_key, (4, D), jnp.float32, -0.5, 0.5)
    return jnp.stack([gains[0], shifts[0], gains[1], shifts[1], shifts[2], shifts[3]])


def block_levels(rng, extent, pieces, smallest, top_value):
    factor_of, own = 1.0, jax.random.fold_in(rng, 6)
    for axis_at, shards_of in pieces:
        heights = jnp.exp(jax.random.uniform(jax.random.fold_in(own, axis_at), (shards_of,), jnp.float32, smallest / len(pieces), top_value / len(pieces)))
        factor_of = factor_of * jnp.repeat(heights, extent[axis_at] // shards_of).reshape([-1 if axis == axis_at else 1 for axis in range(len(extent))])
    return factor_of


def normal_values(rng, shape, scale, limit, pieces=(), kind=jnp.bfloat16):
    loudness = block_levels(rng, shape, pieces, -0.22, 0.18) if pieces else 1.0
    values = jax.random.normal(rng, shape, jnp.float32) * scale * loudness
    return jnp.minimum(jnp.maximum(values, -limit), limit).astype(kind)


def setup_inputs(seed: int = 0) -> dict:
    key_list = jax.random.split(jax.random.key(seed), 21)
    return {
        "tokens": normal_values(key_list[0], (TOKENS, D), 1.0, 6.0, ((0, 8),)),
        "cotangent": normal_values(key_list[1], (TOKENS, D), 1.0, 6.0, ((0, 8),)),
        "qkv_weight": normal_values(key_list[2], (3, D, D), D ** -0.5, 0.21875, ((1, 8), (2, 4)), jnp.float32),
        "out_weight": normal_values(key_list[3], (D, D), (D // 16) ** -0.5, 0.875, ((0, 4), (1, 8)), jnp.float32),
        "up_weight": normal_values(key_list[4], (D, FF), D ** -0.5, 0.21875, ((0, 8), (1, 4)), jnp.float32),
        "down_weight": normal_values(key_list[5], (FF, D), FF ** -0.5, 0.109375, ((0, 4), (1, 8)), jnp.float32),
        "shared_vectors": draw_shared_vectors(jax.random.fold_in(key_list[20], 71), 0),
        "split_vectors": normal_values(key_list[7], (N_TENSOR, (2 * D + FF) // N_TENSOR), 0.3, 1.5, ((0, 4), (1, 8)), jnp.float32),
        "qkv_first": normal_values(key_list[8], (3, D, D), (0.08 * TOKENS ** 0.5), 80.0, ((1, 8), (2, 4)), jnp.float32),
        "qkv_second": jnp.clip(jnp.exp(math.log(100.864) - 2.7725887 * jax.random.uniform(key_list[9], (3, D, D), jnp.float32) ** block_levels(key_list[9], (3, D, D), ((1, 8), (2, 4)), -0.2, 0.2)), 6.304, 100.864),
        "out_first": normal_values(key_list[10], (D, D), (0.016 * TOKENS ** 0.5), 16.0, ((0, 4), (1, 8)), jnp.float32),
        "out_second": jnp.clip(jnp.exp(math.log(4.03456) - 2.7725887 * jax.random.uniform(key_list[11], (D, D), jnp.float32) ** block_levels(key_list[11], (D, D), ((0, 4), (1, 8)), -0.2, 0.2)), 0.25216, 4.03456),
        "up_first": normal_values(key_list[12], (D, FF), (0.033 * TOKENS ** 0.5), 32.0, ((0, 8), (1, 4)), jnp.float32),
        "up_second": jnp.clip(jnp.exp(math.log(18.15552) - 2.7725887 * jax.random.uniform(key_list[13], (D, FF), jnp.float32) ** block_levels(key_list[13], (D, FF), ((0, 8), (1, 4)), -0.2, 0.2)), 1.13472, 18.15552),
        "down_first": normal_values(key_list[14], (FF, D), (0.066 * TOKENS ** 0.5), 64.0, ((0, 4), (1, 8)), jnp.float32),
        "down_second": jnp.clip(jnp.exp(math.log(73.1264) - 2.7795092 * jax.random.uniform(key_list[15], (FF, D), jnp.float32) ** block_levels(key_list[15], (FF, D), ((0, 4), (1, 8)), -0.2, 0.2)), 4.53888, 73.1264),
        "shared_first": normal_values(key_list[16], (6, D), (0.08 * TOKENS ** 0.5), 80.0, ((1, 8),), jnp.float32),
        "shared_second": jnp.clip(jnp.exp(math.log(100.864) - 2.7725887 * jax.random.uniform(key_list[17], (6, D), jnp.float32) ** block_levels(key_list[17], (6, D), ((1, 8),), -0.2, 0.2)), 6.304, 100.864),
        "split_first": normal_values(key_list[18], (N_TENSOR, (2 * D + FF) // N_TENSOR), (0.08 * TOKENS ** 0.5), 80.0, ((0, 4), (1, 8)), jnp.float32),
        "split_second": jnp.clip(jnp.exp(math.log(100.864) - 2.7725887 * jax.random.uniform(key_list[19], (N_TENSOR, (2 * D + FF) // N_TENSOR), jnp.float32) ** block_levels(key_list[19], (N_TENSOR, (2 * D + FF) // N_TENSOR), ((0, 4), (1, 8)), -0.2, 0.2)), 6.304, 100.864),
    }


@jax.custom_vjp
def low(v):
    return lax.optimization_barrier(v.astype(jnp.bfloat16)).astype(jnp.float32)

@jax.custom_vjp
def low_back(v):
    return v

def low_keep(v):
    return (low(v), None)

def low_pass(kept, grad):
    return (grad,)

def back_keep(v):
    return (v, None)

def back_low(kept, grad):
    return (low(grad),)
low.defvjp(low_keep, low_pass)
low_back.defvjp(back_keep, back_low)
EPS_NORM = 1e-06
EPS_ADAM = 1e-08
BETA_ONE = 0.9
BETA_TWO = 0.999
RATE_MATRIX = 0.05
RATE_VECTOR = 0.2
DECAY_MATRIX = 0.05
HIGH = lax.Precision.HIGHEST

def layer_norm(values, gain, shift):
    centre = values - lax.optimization_barrier(jnp.mean(values, axis=-1, keepdims=True))
    spread = lax.optimization_barrier(jnp.mean(centre * centre, axis=-1, keepdims=True))
    return centre * lax.rsqrt(spread + EPS_NORM) * gain + shift

def forward(inputs, qkv_weight, out_weight, up_weight, down_weight, shared, split):
    quarter = D // N_TENSOR
    table = split.reshape(N_TENSOR, quarter, 6)
    query_bias = table[:, :, 0].reshape(D)
    value_bias = table[:, :, 1].reshape(D)
    hidden_bias = table[:, :, 2:].reshape(FF)
    row_count = inputs.shape[0]
    images = row_count // SEQ
    normed = low(layer_norm(inputs, shared[0], shared[1]))
    projected = jnp.einsum('td,cde->cte', normed, low(qkv_weight), precision=HIGH)
    queries = low_back(low(projected[0] + query_bias)).reshape(images, SEQ, HEADS, HEAD)
    key_heads = low_back(low(projected[1])).reshape(images, SEQ, HEADS, HEAD)
    values = low_back(low(projected[2] + value_bias)).reshape(images, SEQ, HEADS, HEAD)
    raw_scores = low_back(jnp.einsum('bqhe,bkhe->bhqk', queries, key_heads, precision=HIGH))
    scores = raw_scores * (1.0 / math.sqrt(HEAD))
    highest = lax.optimization_barrier(jnp.max(scores, axis=-1, keepdims=True))
    exponent = jnp.exp(scores - highest)
    probs = exponent / lax.optimization_barrier(jnp.sum(exponent, axis=-1, keepdims=True))
    attended = jnp.einsum('bhqk,bkhe->bqhe', low(probs), values, precision=HIGH).reshape(row_count, D)
    attended = low_back(low(attended))
    branch = low_back(jnp.dot(attended, low(out_weight), precision=HIGH))
    middle = inputs + branch + shared[4]
    normed_two = low(layer_norm(middle, shared[2], shared[3]))
    hidden_in = low_back(jnp.dot(normed_two, low(up_weight), precision=HIGH) + hidden_bias)
    hidden = low(jax.nn.gelu(hidden_in, approximate=False))
    return middle + jnp.dot(hidden, low(down_weight), precision=HIGH) + shared[5]

def adam_step(weight, gradient, first, second, rate, decay):
    first = BETA_ONE * first + (1.0 - BETA_ONE) * gradient
    second = BETA_TWO * second + (1.0 - BETA_TWO) * gradient * gradient
    corr_one = 1.0 - BETA_ONE ** STEP
    corr_two = 1.0 - BETA_TWO ** STEP
    updated = weight * (1.0 - rate * decay) - rate * (first / corr_one) / (jnp.sqrt(second / corr_two) + EPS_ADAM)
    return (first, second, updated)

def reference(tokens, cotangent, qkv_weight, out_weight, up_weight, down_weight, shared_vectors, split_vectors, qkv_first, qkv_second, out_first, out_second, up_first, up_second, down_first, down_second, shared_first, shared_second, split_first, split_second):
    params = (qkv_weight, out_weight, up_weight, down_weight, shared_vectors, split_vectors)
    block_rows = IMG_DEV * SEQ
    inputs = tokens.astype(jnp.float32).reshape(N_DP, block_rows, D)
    back_rows = cotangent.astype(jnp.float32).reshape(N_DP, block_rows, D)

    def one_block(running, paired):
        block_in, block_back = paired
        result, pullback = jax.vjp(forward, block_in, *params)
        gradients = pullback(block_back)
        running = tuple((total_grad + gradient for total_grad, gradient in zip(running, gradients[1:])))
        return (running, (result.astype(jnp.bfloat16), gradients[0].astype(jnp.bfloat16)))
    starting = tuple((jnp.zeros_like(param) for param in params))
    totals, (outputs, input_grads) = lax.scan(one_block, starting, (inputs, back_rows))
    qkv_new = adam_step(qkv_weight, totals[0], qkv_first, qkv_second, RATE_MATRIX, DECAY_MATRIX)
    out_new = adam_step(out_weight, totals[1], out_first, out_second, RATE_MATRIX, DECAY_MATRIX)
    up_new = adam_step(up_weight, totals[2], up_first, up_second, RATE_MATRIX, DECAY_MATRIX)
    down_new = adam_step(down_weight, totals[3], down_first, down_second, RATE_MATRIX, DECAY_MATRIX)
    shared_new = adam_step(shared_vectors, totals[4], shared_first, shared_second, RATE_VECTOR, 0.0)
    split_new = adam_step(split_vectors, totals[5], split_first, split_second, RATE_VECTOR, 0.0)
    return (outputs.reshape(TOKENS, D), input_grads.reshape(TOKENS, D), qkv_new[0], qkv_new[1], qkv_new[2], out_new[0], out_new[1], out_new[2], up_new[0], up_new[1], up_new[2], down_new[0], down_new[1], down_new[2], shared_new[0], shared_new[1], shared_new[2], split_new[0], split_new[1], split_new[2])
```

```python
import math
from functools import partial

import jax
import jax.numpy as jnp
from jax import lax
from jax.experimental import pallas as pl
from jax.experimental.pallas import tpu as pltpu
from jax.sharding import PartitionSpec as P

HEAD = 64
SEQ = 197
STEP = 10

EPS_NORM = 1e-06
EPS_ADAM = 1e-08
BETA_ONE = 0.9
BETA_TWO = 0.999
RATE_MATRIX = 0.05
RATE_VECTOR = 0.2
DECAY_MATRIX = 0.05

LOW = jnp.bfloat16
WIDE = jnp.float32
MESH = pl.DeviceIdType.MESH
ROWS = 16
BLOCK = 64
STRIP = 32
FAR_STEP = 64
FAR_SENT = 0
MEGA = 1024 * 1024
VMEM = pl.BlockSpec(memory_space=pltpu.VMEM)
ANY = pl.BlockSpec(memory_space=pl.ANY)


def round_up(value, unit):
    return -(-value // unit) * unit


def rem(left, right):
    return left % right if isinstance(left, int) else lax.rem(left, right)


def div(left, right):
    return left // right if isinstance(left, int) else lax.div(left, right)


def position():
    place, z = lax.axis_index("dp"), lax.axis_index("tensor")
    core, chip = rem(place, 2), div(place, 2)
    x, y = rem(chip, 2), div(chip, 2)
    return chip, core, z, y * 2 + (1 - x), (1 - y) * 2 + x, (1 - y) * 2 + (1 - x)


def z_partner(z, step):
    return z + rem(step, 2) * (1 - 2 * rem(z, 2)) + div(step, 2) * (2 - 4 * div(z, 2))


def chunk(n):
    late = div(n + 4, 8)
    return late * (1 + rem(n, 2)), (1 - late) * n + late * div(n - 4, 2)


def greet(wait=True):
    chip, core, z, x_chip, y_chip, _ = position()
    barrier = pltpu.get_barrier_semaphore()
    targets = [(x_chip * 2 + core, z), (y_chip * 2 + core, z), (chip * 2 + 1 - core, z)]
    targets += [(chip * 2 + core, z_partner(z, step)) for step in (1, 2, 3)]
    for target in targets:
        pl.semaphore_signal(barrier, inc=1, device_id=target, device_id_type=MESH)
    if wait:
        pl.semaphore_wait(barrier, len(targets))
    return barrier, len(targets)


def remote(src, dst, send, recv, target):
    return pltpu.make_async_remote_copy(
        src_ref=src, dst_ref=dst, send_sem=send, recv_sem=recv, device_id=target, device_id_type=MESH
    )


class Share:
    pieces = 2

    def __init__(self, part, whole, send, recv, own, far=range(pieces), far_size=None):
        self.far, self.far_size = far, far_size
        chip, core, self.z, _, _, _ = position()
        self.part, self.whole, self.send, self.recv = part, whole, send, recv
        self.here = chip * 2 + core
        self.size = part.shape[0] // self.pieces
        self.own = pltpu.make_async_copy(part, whole.at[self.z], own)
        self.inner = rem(self.z, 2) + div(self.z, 2) == 1

    def copy(self, kind, piece):
        z = self.z
        short = kind in (2, 4) and self.far_size
        rows = pl.ds(piece * self.size, self.far_size if short else self.size)
        block = z_partner(z, (0, 0, 1, 3, 2)[kind])
        src = (self.part if kind < 2 else self.whole.at[block]).at[rows]
        target = z_partner(z, (1, 3, 3, 1, 1)[kind])
        lane = (0, 1, 2, 1, 2)[kind]
        return remote(
            src, self.whole.at[block, rows], self.send.at[kind, piece], self.recv.at[lane, piece],
            (self.here, target),
        )

    def start(self):
        self.own.start()
        for piece in range(self.pieces):
            self.copy(0, piece).start()

        @pl.when(self.inner)
        def _():
            for piece in range(self.pieces):
                self.copy(1, piece).start()

    def pass_on(self, stage):
        near, piece = stage < self.pieces, stage % self.pieces

        @pl.when(self.inner)
        def _():
            if near:
                self.copy(0, piece).wait_recv()
                if piece in self.far:
                    self.copy(2, piece).start()
                self.copy(1, piece).wait_recv()
                self.copy(3, piece).start()
            elif piece in self.far:
                self.copy(2, piece).wait_recv()
                self.copy(4, piece).start()

    def finish(self):
        def each(kinds):
            for kind in kinds:
                for piece in self.far if kind in (2, 4) else range(self.pieces):
                    yield self.copy(kind, piece)

        @pl.when(jnp.logical_not(self.inner))
        def _():
            for copy in each((0, 3, 4)):
                copy.wait_recv()
            for copy in each((0,)):
                copy.wait_send()

        @pl.when(self.inner)
        def _():
            for copy in each(range(5)):
                copy.wait_send()

        self.own.wait()


def share_scratch():
    return [
        pltpu.SemaphoreType.DMA((5, Share.pieces)),
        pltpu.SemaphoreType.DMA((3, Share.pieces)),
        pltpu.SemaphoreType.DMA,
    ]


def dot(left, right, left_dim=1, right_dim=0):
    return lax.dot_general(
        left, right, (((left_dim,), (right_dim,)), ((), ())), preferred_element_type=WIDE
    )


def fill_unit(unit):
    row, column = (lax.broadcasted_iota(jnp.int32, unit.shape, dim) for dim in (0, 1))
    unit[...] = jnp.where(row == column, 1.0, 0.0).astype(LOW)


def flip(value, unit):
    count = value.shape[1]
    return dot(unit[:count, :count], value, 1, 1).astype(LOW)


def block_at(at):
    return pl.ds(pl.multiple_of(at * BLOCK, BLOCK), BLOCK)


def norm_parts(values):
    centre = values - jnp.mean(values, axis=-1, keepdims=True)
    factor = lax.rsqrt(jnp.mean(centre * centre, axis=-1, keepdims=True) + EPS_NORM)
    return centre * factor, factor


def norm_backward(grad_out, unit, factor, gain):
    scaled = grad_out * gain
    return factor * (
        scaled
        - jnp.mean(scaled, axis=-1, keepdims=True)
        - unit * jnp.mean(scaled * unit, axis=-1, keepdims=True)
    )


def fold(values):
    return jnp.sum(values.reshape(values.shape[0] // 8, 8, values.shape[1]), axis=0)


def attend(image, qkv, attended, mask, unit, turn, kept=None):
    padded, width = mask.shape[0], attended.shape[1]
    scale = 1.0 / math.sqrt(HEAD)
    spot = pl.ds(pl.multiple_of(image * padded, padded), padded)
    turn[0] = flip(qkv[spot, 2 * width : 3 * width], unit)
    for head in range(width // HEAD):
        lanes = head * HEAD
        query = qkv[spot, lanes : lanes + HEAD]
        key = qkv[spot, width + lanes : width + lanes + HEAD]
        scores = dot(key, query, 1, 1) + mask[...]
        highest = jnp.max(scores, axis=0, keepdims=True)
        exponent = jnp.exp((scores - highest) * scale)
        total = jnp.sum(exponent, axis=0, keepdims=True)
        prob = (exponent * (1.0 / total)).astype(LOW)
        if kept is not None:
            kept[image, head] = prob
        turn[1, lanes : lanes + HEAD, :] = dot(turn[0, lanes : lanes + HEAD, :], prob).astype(LOW)
    attended[spot, :] = flip(turn[1], unit)


def fill_mask(mask):
    mask[...] = jnp.where(lax.broadcasted_iota(jnp.int32, mask.shape, 0) < SEQ, 0.0, -1e30)


def gelu_parts(value):
    cdf = 0.5 * (1.0 + lax.erf(value * (1.0 / math.sqrt(2.0))))
    return cdf, jnp.exp(-0.5 * value * value) * (1.0 / math.sqrt(2.0 * math.pi))


class Rows:
    def __init__(self, src, window, sems, begin, images, padded):
        self.src, self.window, self.sems = src, window, sems
        self.begin, self.images, self.padded = begin, images, padded

    def copy(self, image):
        begin = (self.begin + image) * SEQ
        last = self.src.shape[0] - SEQ
        aligned = div(begin, ROWS) * ROWS - ROWS * div(begin, last)
        rows = pl.ds(pl.multiple_of(aligned, ROWS), self.window.shape[1])
        copy = pltpu.make_async_copy(self.src.at[rows], self.window.at[image], self.sems.at[image])
        return copy, begin - aligned

    def fetch(self):
        for image in range(self.images):
            self.copy(image)[0].start()

    def place(self, dst):
        span, padded = self.window.shape[1], self.padded

        @pl.loop(0, self.images)
        def _(image):
            copy, shift = self.copy(image)
            copy.wait()
            moved = pltpu.roll(self.window[image].astype(WIDE), rem(span - shift, span), axis=0)[:padded]
            inside = lax.broadcasted_iota(jnp.int32, (padded, 1), 0) < SEQ
            spot = pl.ds(pl.multiple_of(image * padded, padded), padded)
            dst[spot, :] = jnp.where(inside, moved, 0.0).astype(LOW)


def far_block(z, tensors):
    return (tensors - 1) * (1 - div(z, tensors // 2))


def pack_images(values, work, images, padded):
    for image in range(images):
        work[image * SEQ : (image + 1) * SEQ, :] = values[image * padded : image * padded + SEQ, :]


def arrange(raw, shard, vec, slab, width):
    qkv, out, up, down_t, shared, split = raw
    for at in range(3):
        shard[0, :, at * width : (at + 1) * width] = qkv[at].astype(LOW)
    shard[0, :, 3 * width :] = out[...].T.astype(LOW)
    shard[1] = up[...].astype(LOW)
    shard[2] = down_t[...].astype(LOW)
    vec[...] = jnp.zeros_like(vec)
    vec[:6, :slab] = shared[...]
    count = split.shape[1]
    groups = count // 6
    column = jnp.broadcast_to(split[...], (8, count)).T[:, :1]
    row, lane = (lax.broadcasted_iota(jnp.int32, (count, 128), dim) for dim in (0, 1))
    attention = jnp.where(lane < groups, 6 * lane, jnp.where(lane < 2 * groups, 6 * (lane - groups) + 1, -1))
    hidden = jnp.where(lane < 4 * groups, 6 * div(lane, 4) + 2 + rem(lane, 4), -1)
    for at, wanted in ((6, attention), (7, hidden)):
        vec[at : at + 1, :] = jnp.sum(jnp.where(row == wanted, column, 0.0), axis=0, keepdims=True)


def forward_kernel(
    tokens, cotangent, *refs, linked,
):
    count = 6 if linked else 2
    forward_body(tokens, cotangent, refs[:count], *refs[count:], linked=linked)


def forward_body(
    tokens, cotangent, sources,
    packed, weights_out, own_out, back_out, back_t_out, gains_out, biases_out,
    normed_out, qkv_out, probs_out, attended_out, middle_out, two_out, hidden_out, slope_out,
    held, vec_held, gains, biases, window, own, back, back_t,
    normed, qkv, probs, attended, middle, two, hidden, slope, work, feed,
    mask, unit, turn, in_sem, row_sem, out_sem, act_sem, weight_sem, vec_send, vec_recv, send, recv, *own_parts,
    linked,
):
    tensors = held.shape[1]
    model, hidden_width = own.shape[1], held.shape[-1]
    width = hidden_width // 4
    heads = width // HEAD
    images, padded = probs.shape[1], probs.shape[-1]
    rows = images * padded
    scale = 1.0 / math.sqrt(HEAD)
    chunks = 3 * tensors
    z = lax.axis_index("tensor")

    own_tokens = Rows(tokens, window, row_sem, z * images, images, padded)
    own_cotangent = Rows(cotangent, window, row_sem, z * images, images, padded)

    def fill_constants():
        fill_unit(unit)
        fill_mask(mask)
        biases[...] = jnp.zeros_like(biases)

    own_tokens.fetch()

    if linked:
        chip, core, _, x_chip, y_chip, far_chip = position()
        x_dev, y_dev, other = (x_chip * 2 + core, z), (y_chip * 2 + core, z), (chip * 2 + 1 - core, z)
        half = held.shape[4] // 2
        weights, vec, *raw = own_parts
        raw_copies = [
            pltpu.make_async_copy(src, dst, vec_send.at[div(at, 3), rem(at, 3)])
            for at, (src, dst) in enumerate(zip(sources, raw))
        ]
        for copy in raw_copies:
            copy.start()
        barrier = greet(wait=False)
        for copy in raw_copies:
            copy.wait()
        arrange(raw, weights, vec, held.shape[4], width)
        pl.semaphore_wait(*barrier)

        def link(n, kind):
            group, step = chunk(n)
            t = z_partner(z, step)
            sems = (send.at[n, kind], recv.at[n, kind])
            spot = held.at[group, t, chip, core]
            if kind == 0:
                to = (chip * 2 + core, t)
                return remote(weights.at[group], held.at[group, z, chip, core], *sems, to)
            if kind == 1:
                return remote(spot, spot, *sems, x_dev)
            if kind == 2:
                return remote(spot, spot, *sems, y_dev)
            if kind == 3:
                spot = held.at[group, t, x_chip, core, pl.ds(0, half)]
                return remote(spot, spot, *sems, y_dev)
            if kind == 4:
                spot = held.at[group, t, y_chip, core, pl.ds(half, half)]
                return remote(spot, spot, *sems, x_dev)
            spot = held.at[group, t, :, core]
            return remote(spot, spot, *sems, other)

        def vec_link(step, kind):
            t = z_partner(z, step)
            sems = (vec_send.at[step, kind], vec_recv.at[step, kind])
            if kind == 0:
                return remote(vec, vec_held.at[z, chip, core], *sems, (chip * 2 + core, t))
            spot = vec_held.at[t, x_chip if kind == 3 else chip, core]
            if kind == 5:
                spot = vec_held.at[t, :, core]
            return remote(spot, spot, *sems, {1: x_dev, 2: y_dev, 3: y_dev, 5: other}[kind])

        own_copies = [
            pltpu.make_async_copy(weights.at[group], held.at[group, z, chip, core], in_sem.at[group, 0])
            for group in range(3)
        ] + [pltpu.make_async_copy(vec, vec_held.at[z, chip, core], in_sem.at[3, 0])]
        for copy in own_copies:
            copy.start()
        for step in (1, 2, 3):
            vec_link(step, 0).start()
        for n in range(chunks):
            if chunk(n)[1]:
                link(n, 0).start()

        def first(n):
            if isinstance(n, int):
                if chunk(n)[1]:
                    link(n, 0).wait_recv()
            else:

                @pl.when(chunk(n)[1] > 0)
                def _():
                    link(n, 0).wait_recv()

            link(n, 1).start()
            link(n, 2).start()

        def second(n):
            link(n, 1).wait_recv()
            link(n, 3).start()
            link(n, 2).wait_recv()
            link(n, 4).start()

        def third(n):
            link(n, 3).wait_recv()
            link(n, 4).wait_recv()
            link(n, 5).start()

        def arrived(n):
            link(n, 5).wait_recv()

        def serve(n):
            first(n + 2)
            second(n)
            third(n - 2)

        for copy in own_copies:
            copy.wait()
        first(0)
        for step in range(4):
            if step:
                vec_link(step, 0).wait_recv()
            vec_link(step, 1).start()
            vec_link(step, 2).start()
        own_tokens.place(own)
        own_cotangent.fetch()
        first(1)
        for step in range(4):
            vec_link(step, 1).wait_recv()
            vec_link(step, 3).start()
        second(0)
        fill_constants()
        for step in range(4):
            vec_link(step, 2).wait_recv()
            vec_link(step, 3).wait_recv()
            vec_link(step, 5).start()
        third(0)
        first(2)
        own_cotangent.place(back)
        back_t[...] = back[...].T
        second(1)
        first(3)
        for step in range(4):
            vec_link(step, 5).wait_recv()
    else:
        weights, vec = sources

        def local(n):
            group, step = chunk(n)
            return pltpu.make_async_copy(
                weights.at[group, step], held.at[group, step, 0, 0], in_sem.at[group, step]
            )

        for n in range(chunks):
            local(n).start()
        copy = pltpu.make_async_copy(vec, vec_held, in_sem.at[3, 0])
        copy.start()
        copy.wait()

        def arrived(n):
            local(n).wait()

        own_tokens.place(own)
        own_cotangent.fetch()
        fill_constants()
        own_cotangent.place(back)
        back_t[...] = back[...].T

    def tensor_at(step):
        return z_partner(z, step) if linked else step

    def keep_weights(n):
        group, step = chunk(n)
        t = tensor_at(step)
        return pltpu.make_async_copy(held.at[group, t], weights_out.at[group, t], weight_sem.at[n])

    def ready(n):
        arrived(n)
        if linked:
            keep_weights(n).start()

    def save(at, src, dst):
        return pltpu.make_async_copy(src, dst, out_sem.at[at])

    places = vec_held.shape[1] * vec_held.shape[2]
    slab, share = model // places, width // places

    @pl.loop(0, tensors)
    def _(t):
        for place in range(places):
            piece = vec_held[t, place // 2, place % 2]
            gains[t, :, place * slab : (place + 1) * slab] = piece[:, :slab]
            biases[t, :, place * share : (place + 1) * share] = piece[:, :share]
            begin = 2 * width + place * share
            biases[t, :, begin : begin + share] = piece[:, share : 2 * share]

    saves = [save(8, own, own_out), save(9, gains, gains_out), save(10, back, back_out)]
    saves += [save(11, biases, biases_out), save(12, back_t, back_t_out)]
    for copy in saves:
        copy.start()

    @pl.loop(0, rows // BLOCK)
    def _(at):
        block = block_at(at)
        inputs = own[block, :].astype(WIDE)
        unit, _ = norm_parts(inputs)
        normed[block, :] = (unit * gains[0, 0:1, :] + gains[0, 1:2, :]).astype(LOW)
        middle[block, :] = inputs + gains[0, 4:5, :]

    saves.append(save(0, normed, normed_out))
    saves[-1].start()

    @pl.loop(0, tensors)
    def _(step):
        t = tensor_at(step)
        ready(step)
        wide = held[0, t, :, :, :, : 3 * width].reshape(model, 3 * width)
        qkv[t] = (dot(normed[...], wide) + biases[t, 6:7, :]).astype(LOW)

        @pl.loop(0, 2)
        def _(part):
            for at in range(images // 2):
                image = part * (images // 2) + at
                attend(image, qkv.at[t], attended.at[t], mask, unit, turn.at[at], probs.at[t])

            if linked:

                @pl.when(jnp.logical_and(part == 0, step == 0))
                def _():
                    first(4)
                    second(2)

                @pl.when(jnp.logical_and(part == 0, step == 1))
                def _():
                    serve(4)

                @pl.when(part == 1)
                def _():
                    serve(3 + step + div(step + 3, 4))

        out = held[0, t, :, :, :, 3 * width :].reshape(model, width)
        middle[...] += dot(attended[t], out, 1, 1)

    saves += [
        save(1, qkv, qkv_out),
        save(2, probs, probs_out),
        save(3, attended, attended_out),
        save(4, middle, middle_out),
    ]
    for copy in saves[-4:]:
        copy.start()

    @pl.loop(0, rows // BLOCK)
    def _(at):
        block = block_at(at)
        values = middle[block, :]
        unit, _ = norm_parts(values)
        two[block, :] = (unit * gains[0, 2:3, :] + gains[0, 3:4, :]).astype(LOW)
        feed[block, :] = values + gains[0, 5:6, :]

    saves.append(save(5, two, two_out))
    saves[-1].start()

    half_rows, wide_lanes = rows // 2, 256
    halves = [pl.ds(0, half_rows), pl.ds(half_rows, half_rows)]

    def keep_acts(step):
        t = tensor_at(step)
        return [
            pltpu.make_async_copy(src.at[t], dst.at[t], act_sem.at[at, step])
            for at, (src, dst) in enumerate(((hidden, hidden_out), (slope, slope_out)))
        ]

    def up_part(half, step, lanes):
        weight = held[1, tensor_at(step), :, :, :, lanes].reshape(model, wide_lanes)
        work[halves[half], lanes] = dot(two[halves[half], :], weight)

    def act_part(half, step, at):
        t = tensor_at(step)
        block = pl.ds(half * half_rows + at * STRIP, STRIP)
        value = work[block, :] + gains[t, 7:8, :]
        cdf, density = gelu_parts(value)
        hidden[t, block, :] = (value * cdf).astype(LOW)
        slope[t, block, :] = (cdf + value * density).astype(LOW)

    def down_part(half, step, lanes):
        t = tensor_at(step)
        weight = held[2, t].reshape(model, hidden_width)[lanes]
        feed[halves[half], lanes] += dot(hidden[t, halves[half], :], weight, 1, 1)

    def together(up=None, act=None, down=None):
        lanes = [slice(at, at + wide_lanes) for at in range(0, hidden_width, wide_lanes)]
        products = [partial(up_part, *up, lane) for lane in lanes] if up else []
        products += [partial(down_part, *down, lane) for lane in lanes] if down else []
        acts = [partial(act_part, *act, at) for at in range(half_rows // STRIP)] if act else []
        every = -(-len(acts) // max(len(products), 1))
        for at, product in enumerate(products):
            product()
            for part in acts[at * every : (at + 1) * every]:
                part()
        for part in acts[len(products) * every :]:
            part()

    ready(tensors)
    together(up=(0, 0))
    if linked:
        serve(8)
    together(up=(1, 0), act=(0, 0))
    if linked:
        serve(9)

    @pl.loop(1, tensors)
    def _(step):
        ready(2 * step + 3)
        ready(2 * step + 4)
        together(up=(0, step), act=(1, step - 1), down=(0, step - 1))
        for copy in keep_acts(step - 1):
            copy.start()
        if linked:

            @pl.when(step == 1)
            def _():
                second(10)
                third(8)

            @pl.when(step == 2)
            def _():
                third(10)

        together(up=(1, step), act=(0, step), down=(1, step - 1))
        if linked:

            @pl.when(step == 1)
            def _():
                second(11)
                third(9)

            @pl.when(step == 2)
            def _():
                third(11)

    last = tensors - 1
    ready(chunks - 1)
    together(act=(1, last), down=(0, last))
    for copy in keep_acts(last):
        copy.start()
    together(down=(1, last))
    for step in range(tensors):
        saves += keep_acts(step)
    pack_images(feed, work, images, padded)
    packed[...] = work[: packed.shape[0], :].astype(LOW)
    for copy in saves:
        copy.wait()
    if linked:
        for step in range(4):
            for kind in (0, 1, 2, 3, 5):
                if kind or step:
                    vec_link(step, kind).wait_send()

        @pl.loop(0, chunks)
        def _(n):
            @pl.when(chunk(n)[1] > 0)
            def _():
                link(n, 0).wait_send()

            for kind in range(1, 6):
                link(n, kind).wait_send()
            keep_weights(n).wait()


def forward(tokens, cotangent, sources, images, width, tensors, places, linked):
    model, hidden_width = tokens.shape[1], 4 * width
    padded, heads = round_up(SEQ, ROWS), width // HEAD
    rows, packed_rows = images * padded, round_up(images * SEQ, 2 * ROWS)
    if linked:
        blocks = (3, tensors, places // 2, 2, model // places, hidden_width)
    else:
        blocks = (3, tensors, 1, 1, model, hidden_width)
    kept = (
        ((rows, model), LOW),
        ((tensors, rows, 3 * width), LOW),
        ((tensors, images, heads, padded, padded), LOW),
        ((tensors, rows, width), LOW),
        ((rows, model), WIDE),
        ((rows, model), LOW),
        ((tensors, rows, hidden_width), LOW),
        ((tensors, rows, hidden_width), LOW),
    )
    outs = (
        ((packed_rows, model), LOW),
        (blocks if linked else (8, 128), LOW),
        ((rows, model), LOW),
        ((rows, model), LOW),
        ((model, rows), LOW),
        ((tensors, 8, model), WIDE),
        ((tensors, 8, 3 * width), WIDE),
    ) + kept
    dma = pltpu.SemaphoreType.DMA
    own_parts = []
    if linked:
        own_parts = [pltpu.VMEM((3, model // places, hidden_width), LOW), pltpu.VMEM((8, 128), WIDE)]
        own_parts += [pltpu.VMEM(source.shape, WIDE) for source in sources]
    return pl.pallas_call(
        partial(forward_kernel, linked=linked),
        out_shape=[jax.ShapeDtypeStruct(shape, dtype) for shape, dtype in outs],
        in_specs=[ANY] * (2 + len(sources)),
        out_specs=[VMEM] + [ANY] * (len(outs) - 1),
        scratch_shapes=[
            pltpu.VMEM(blocks, LOW),
            pltpu.VMEM((tensors, places // 2, 2, 8, 128), WIDE),
            pltpu.VMEM((tensors, 8, model), WIDE),
            pltpu.VMEM((tensors, 8, 3 * width), WIDE),
            pltpu.VMEM((images, padded + ROWS, model), LOW),
            pltpu.VMEM((rows, model), LOW),
            pltpu.VMEM((rows, model), LOW),
            pltpu.VMEM((model, rows), LOW),
        ]
        + [pltpu.VMEM(shape, dtype) for shape, dtype in kept]
        + [
            pltpu.VMEM((rows, hidden_width), WIDE),
            pltpu.VMEM((rows, model), WIDE),
            pltpu.VMEM((padded, padded), WIDE),
            pltpu.VMEM((padded, padded), LOW),
            pltpu.VMEM((images // 2, 2, width, padded), LOW),
            dma((4, tensors)),
            dma((images,)),
            dma((13,)),
            dma((2, tensors)),
            dma((3 * tensors,)),
            dma((4, 6)),
            dma((4, 6)),
            dma((3 * tensors, 6)),
            dma((3 * tensors, 6)),
        ]
        + own_parts,
        compiler_params=pltpu.CompilerParams(
            vmem_limit_bytes=58 * MEGA, has_side_effects=True, **({"collective_id": 0} if linked else {})
        ),
        name="forward",
    )(tokens, cotangent, *sources)


def chain_kernel(
    packed, tokens_in, cotangent, cot_t_in, gains, weights, qkv_in, probs_in, middle_in, slope_in, hidden_in,
    packed_grad, block_out, hidden_back_out, back_low_out, qkv_back_out, vec_grads, down_grads,
    tokens, cot_t, mixed, stream, slopes, acts, staged, qkv, probs, middle, work, total, back, back_low, hidden_back, attended_back,
    qkv_back, rows_eight, bias_rows, unit, turn, in_sem, stream_sem, out_sem, down_sem, *share_sems,
    linked,
):
    rows, model = cotangent.shape
    tensors, hidden_width = weights.shape[1], weights.shape[-1]
    width = hidden_width // 4
    heads = width // HEAD
    images, padded = probs.shape[1], probs.shape[-1]
    scale = 1.0 / math.sqrt(HEAD)
    places = vec_grads.shape[1]
    slab, part = model // places, width // places

    if linked:
        greet()
        shared = Share(packed, block_out, *share_sems, far=())
        shared.start()

    def fetch(t):
        slot = rem(t, 2)
        pairs = (
            (weights.at[2, t], stream.at[slot, 0]),
            (slope_in.at[t], slopes.at[slot]),
            (weights.at[1, t], stream.at[slot, 1]),
            (hidden_in.at[t], acts.at[slot]),
        )
        return [
            pltpu.make_async_copy(src, dst, stream_sem.at[slot, at]) for at, (src, dst) in enumerate(pairs)
        ]

    for copy in fetch(0):
        copy.start()
    turned = pltpu.make_async_copy(cot_t_in, cot_t, in_sem.at[5])
    turned.start()
    pairs = (
        (middle_in, middle), (weights.at[0], mixed), (qkv_in, qkv), (probs_in, probs), (tokens_in, tokens),
    )
    loads = [pltpu.make_async_copy(src, dst, in_sem.at[at]) for at, (src, dst) in enumerate(pairs)]
    for copy in loads:
        copy.start()
    total[...] = jnp.zeros_like(total)
    rows_eight[...] = jnp.zeros_like(rows_eight)
    fill_unit(unit)

    def keep_down(t):
        slot = rem(t, 2)
        return pltpu.make_async_copy(staged.at[slot], down_grads.at[t], down_sem.at[slot])

    def keep_hidden(t):
        slot = rem(t, 2)
        return pltpu.make_async_copy(hidden_back.at[slot], hidden_back_out.at[t], out_sem.at[slot])

    @pl.loop(0, tensors)
    def _(t):
        slot = rem(t, 2)

        @pl.when(t + 1 < tensors)
        def _():
            for copy in fetch(t + 1):
                copy.start()

        @pl.when(t > 1)
        def _():
            keep_hidden(t - 2).wait()
            keep_down(t - 2).wait()

        copies = fetch(t)
        copies[0].wait()
        work[...] = dot(cotangent[...], stream[slot, 0].reshape(model, hidden_width))
        copies[1].wait()

        def through(at, sums):
            block = block_at(at)
            low = (work[block, :] * slopes[slot, block, :].astype(WIDE)).astype(LOW)
            hidden_back[slot, block, :] = low
            return sums + fold(low.astype(WIDE))

        sums = lax.fori_loop(0, rows // BLOCK, through, jnp.zeros((8, hidden_width), WIDE))
        rows_eight[t, 7:8, :] = jnp.sum(sums, axis=0, keepdims=True)
        keep_hidden(t).start()
        copies[2].wait()
        total[...] += dot(hidden_back[slot], stream[slot, 1].reshape(model, hidden_width), 1, 1)
        copies[3].wait()

        @pl.when(t == 0)
        def _():
            turned.wait()

        staged[slot] = dot(cot_t[...], acts[slot]).astype(LOW).reshape(staged.shape[1:])
        keep_down(t).start()
        if linked:

            @pl.when(t == tensors // 2)
            def _():
                shared.pass_on(0)
    loads[0].wait()

    def second_norm(at, sums):
        block = block_at(at)
        unit, factor = norm_parts(middle[block, :])
        grad_out = total[block, :]
        from_above = cotangent[block, :].astype(WIDE)
        value = from_above + norm_backward(grad_out, unit, factor, gains[0, 2:3, :])
        back[block, :] = value
        back_low[block, :] = value.astype(LOW)
        parts = (grad_out * unit, grad_out, value, from_above)
        return tuple(old + fold(part) for old, part in zip(sums, parts))

    zero = jnp.zeros((8, model), WIDE)
    sums = lax.fori_loop(0, rows // BLOCK, second_norm, (zero,) * 4)

    def shared_sum(row, value):
        row_sum = jnp.sum(value, axis=0, keepdims=True)
        for t in range(tensors):
            rows_eight[t, row : row + 1, :] = row_sum

    for at, value in enumerate(sums):
        shared_sum(at + 2, value)
    keep_back = pltpu.make_async_copy(back_low, back_low_out, out_sem.at[2])
    keep_back.start()
    if linked:
        shared.pass_on(1)
    for copy in loads[1:]:
        copy.wait()
    total[...] = jnp.zeros_like(total)
    for slot in range(2):
        keep_hidden(slot).wait()
        keep_down(slot).wait()

    def keep_qkv(t):
        slot = rem(t, 2)
        return pltpu.make_async_copy(qkv_back.at[slot], qkv_back_out.at[t], out_sem.at[slot])

    @pl.loop(0, tensors)
    def _(t):
        slot = rem(t, 2)

        @pl.when(t > 1)
        def _():
            keep_qkv(t - 2).wait()

        out = mixed[t, :, :, :, 3 * width :].reshape(model, width)
        attended_back[...] = dot(back_low[...], out).astype(LOW)

        def attend_back(image, turn):
            spot = pl.ds(pl.multiple_of(image * padded, padded), padded)
            turn[0] = flip(qkv[t, spot, width : 2 * width], unit)
            for head in range(heads):
                lanes = head * HEAD
                query = qkv[t, spot, lanes : lanes + HEAD]
                value = qkv[t, spot, 2 * width + lanes : 2 * width + lanes + HEAD]
                grad = attended_back[spot, lanes : lanes + HEAD]
                prob_low = probs[t, image, head]
                prob = prob_low.astype(WIDE)
                weighted = prob * dot(value, grad, 1, 1)
                score_back = weighted - prob * jnp.sum(weighted, axis=0, keepdims=True)
                score_back = (score_back * scale).astype(LOW)
                query_back = dot(turn[0, lanes : lanes + HEAD, :], score_back)
                turn[1, lanes : lanes + HEAD, :] = query_back.astype(LOW)
                begin = width + lanes
                qkv_back[slot, spot, begin : begin + HEAD] = dot(score_back, query).astype(LOW)
                begin = 2 * width + lanes
                qkv_back[slot, spot, begin : begin + HEAD] = dot(prob_low, grad).astype(LOW)

            qkv_back[slot, spot, :width] = flip(turn[1], unit)

        @pl.loop(0, images // 2)
        def _(pair):
            for at in range(2):
                attend_back(2 * pair + at, turn.at[at])

        keep_qkv(t).start()
        bias_rows[t] = jnp.sum(qkv_back[slot].astype(WIDE), axis=0, keepdims=True)
        wide = mixed[t, :, :, :, : 3 * width].reshape(model, 3 * width)
        total[...] += dot(qkv_back[slot], wide, 1, 1)
    def first_norm(at, sums):
        block = block_at(at)
        unit, factor = norm_parts(tokens[block, :].astype(WIDE))
        grad_out = total[block, :]
        back[block, :] += norm_backward(grad_out, unit, factor, gains[0, 0:1, :])
        parts = (grad_out * unit, grad_out)
        return tuple(old + fold(part) for old, part in zip(sums, parts))

    sums = lax.fori_loop(0, rows // BLOCK, first_norm, (zero,) * 2)
    for at, value in enumerate(sums):
        shared_sum(at, value)
    pack_images(back, work, images, padded)
    packed_grad[...] = work[: packed_grad.shape[0], :].astype(LOW)

    vec_grads[...] = jnp.zeros_like(vec_grads)

    @pl.loop(0, tensors)
    def _(t):
        for place in range(places):
            vec_grads[t, place, :, :slab] = rows_eight[t, :, place * slab : (place + 1) * slab]
            vec_grads[t, place, 6:7, :part] = bias_rows[t, :, place * part : (place + 1) * part]
            begin = 2 * width + place * part
            vec_grads[t, place, 6:7, part : 2 * part] = bias_rows[t, :, begin : begin + part]

    keep_back.wait()
    for slot in range(2):
        keep_qkv(slot).wait()
    if linked:
        shared.finish()


def chain(packed, tokens, cotangent, cot_t, gains, weights, qkv, probs, middle, slope, hidden, places, linked):
    rows, model = tokens.shape
    tensors, hidden_width = weights.shape[1], weights.shape[-1]
    width = hidden_width // 4
    dma = pltpu.SemaphoreType.DMA
    whole = (tensors,) + packed.shape if linked else (8, 128)
    outs = (
        (packed.shape, LOW),
        (whole, LOW),
        ((tensors, rows, hidden_width), LOW),
        ((rows, model), LOW),
        ((tensors, rows, 3 * width), LOW),
        ((tensors, places, 8, 128), WIDE),
        (weights.shape[1:], LOW),
    )
    return pl.pallas_call(
        partial(chain_kernel, linked=linked),
        out_shape=[jax.ShapeDtypeStruct(shape, dtype) for shape, dtype in outs],
        in_specs=[ANY, ANY, VMEM, ANY, VMEM] + [ANY] * 6,
        out_specs=[VMEM] + [ANY] * 4 + [VMEM, ANY],
        scratch_shapes=[
            pltpu.VMEM((rows, model), LOW),
            pltpu.VMEM((model, rows), LOW),
            pltpu.VMEM(weights.shape[1:], LOW),
            pltpu.VMEM((2, 2) + weights.shape[2:], LOW),
            pltpu.VMEM((2, rows, hidden_width), LOW),
            pltpu.VMEM((2, rows, hidden_width), LOW),
            pltpu.VMEM((2,) + weights.shape[2:], LOW),
            pltpu.VMEM(qkv.shape, LOW),
            pltpu.VMEM(probs.shape, LOW),
            pltpu.VMEM((rows, model), WIDE),
            pltpu.VMEM((rows, hidden_width), WIDE),
            pltpu.VMEM((rows, model), WIDE),
            pltpu.VMEM((rows, model), WIDE),
            pltpu.VMEM((rows, model), LOW),
            pltpu.VMEM((2, rows, hidden_width), LOW),
            pltpu.VMEM((rows, width), LOW),
            pltpu.VMEM((2, rows, 3 * width), LOW),
            pltpu.VMEM((tensors, 8, model), WIDE),
            pltpu.VMEM((tensors, 1, 3 * width), WIDE),
            pltpu.VMEM(probs.shape[-2:], LOW),
            pltpu.VMEM((2, 2, width, probs.shape[-1]), LOW),
            dma((6,)),
            dma((2, 4)),
            dma((3,)),
            dma((2,)),
        ]
        + (share_scratch() if linked else []),
        compiler_params=pltpu.CompilerParams(
            vmem_limit_bytes=58 * MEGA, has_side_effects=True, **({"collective_id": 1} if linked else {})
        ),
        name="chain",
    )(packed, tokens, cotangent, cot_t, gains, weights, qkv, probs, middle, slope, hidden)


class Far:
    def __init__(
        self, tokens, weights, gains, biases, out,
        held, window, inputs, normed, qkv, attended, middle, two, work, hidden, packed, mask, unit, turn,
        weight_sem, row_sem, out_sem,
    ):
        self.weights, self.gains, self.biases = weights, gains, biases
        self.held, self.weight_sem = held, weight_sem
        self.inputs, self.normed, self.qkv, self.attended = inputs, normed, qkv, attended
        self.middle, self.two, self.work, self.hidden = middle, two, work, hidden
        self.packed, self.mask, self.unit, self.turn = packed, mask, unit, turn
        self.tensors = weights.shape[1]
        self.rows, self.model = inputs.shape
        self.hidden_width = weights.shape[-1]
        self.width = self.hidden_width // 4
        self.padded = mask.shape[0]
        self.images = self.rows // self.padded
        block = far_block(lax.axis_index("tensor"), self.tensors)
        first = block * (self.images + FAR_SENT) + FAR_SENT
        self.source = Rows(tokens, window, row_sem, first, self.images, self.padded)
        self.store = pltpu.make_async_copy(packed, out, out_sem)

    def weight(self, at):
        group, t = chunk(at)
        slot = rem(at, 2)
        return pltpu.make_async_copy(self.weights.at[group, t], self.held.at[slot], self.weight_sem.at[slot])

    def start(self):
        self.source.fetch()
        self.weight(0).start()
        self.weight(1).start()

    def each_block(self, body):
        @pl.loop(0, self.rows // FAR_STEP)
        def _(at):
            body(pl.ds(pl.multiple_of(at * FAR_STEP, FAR_STEP), FAR_STEP))

    def first_norm(self):
        fill_unit(self.unit)
        fill_mask(self.mask)
        self.source.place(self.inputs)

        def body(block):
            inputs = self.inputs[block, :].astype(WIDE)
            unit, _ = norm_parts(inputs)
            self.normed[block, :] = (unit * self.gains[0, 0:1, :] + self.gains[0, 1:2, :]).astype(LOW)
            self.middle[block, :] = inputs + self.gains[0, 4:5, :]

        self.each_block(body)

    def attention(self, t):
        width = self.width
        slot = rem(t, 2)
        self.weight(t).wait()
        weight = self.held[slot, :, :, :, : 3 * width].reshape(self.model, 3 * width)
        self.qkv[...] = (dot(self.normed[...], weight) + self.biases[t, 6:7, :]).astype(LOW)

        @pl.loop(0, self.images // 2)
        def _(pair):
            for at in range(2):
                attend(2 * pair + at, self.qkv, self.attended, self.mask, self.unit, self.turn.at[at])

        weight = self.held[slot, :, :, :, 3 * width :].reshape(self.model, width)
        self.middle[...] += dot(self.attended[...], weight, 1, 1)
        self.weight(t + 2).start()

    def second_norm(self):
        def body(block):
            values = self.middle[block, :]
            unit, _ = norm_parts(values)
            self.two[block, :] = (unit * self.gains[0, 2:3, :] + self.gains[0, 3:4, :]).astype(LOW)
            self.middle[block, :] = values + self.gains[0, 5:6, :]

        self.each_block(body)

    def up(self, t):
        at = self.tensors + 2 * t
        self.weight(at).wait()
        self.work[...] = dot(self.two[...], self.held[rem(at, 2)].reshape(self.model, self.hidden_width))

        @pl.when(t + 1 < self.tensors)
        def _():
            self.weight(at + 2).start()

        def body(block):
            value = self.work[block, :] + self.gains[t, 7:8, :]
            self.hidden[block, :] = (value * gelu_parts(value)[0]).astype(LOW)

        self.each_block(body)

    def down(self, t):
        at = self.tensors + 2 * t + 1
        self.weight(at).wait()
        weight = self.held[rem(at, 2)].reshape(self.model, self.hidden_width)
        self.middle[...] += dot(self.hidden[...], weight, 1, 1)

        @pl.when(t + 1 < self.tensors)
        def _():
            self.weight(at + 2).start()

    def step(self, n):
        tensors = self.tensors

        @pl.when(n == 0)
        def _():
            self.first_norm()

        @pl.when(jnp.logical_and(n > 0, n <= tensors))
        def _():
            self.attention(n - 1)

        @pl.when(n == tensors + 1)
        def _():
            self.second_norm()

        @pl.when(jnp.logical_and(n > tensors + 1, n <= 2 * tensors + 1))
        def _():
            self.up(n - tensors - 2)
            self.down(n - tensors - 2)

        @pl.when(n == 2 * tensors + 2)
        def _():
            self.finish()

    def finish(self):
        pack_images(self.middle, self.work, self.images, self.padded)
        self.packed[...] = self.work[: self.packed.shape[0], :].astype(LOW)
        self.store.start()

    def wait(self):
        self.store.wait()


def grads_kernel(
    packed, vec_grads, normed_in, two_in, back_in, qkv_back_in, attended_in, hidden_back_in, down_grads,
    tokens, weights, gains, biases,
    tokens_grad, total_out, vec_out, far_out,
    flat, normed_t, two_t, back_t, acts, mixed_acts, attended_acts, staged,
    pair, x_half, y_half, x_full, y_full, z_sum, vec_pair, vec_x, vec_y, vec_z,
    in_sem, act_sem, keep_sem, vec_send, vec_recv, send, recv, *more,
    linked,
):
    share_sems, far_scratch = more[:3], more[3:]
    tensors, rows, hidden_width = hidden_back_in.shape
    width = hidden_width // 4
    chunks = 3 * tensors
    z = lax.axis_index("tensor")

    def tensor_at(step):
        return z_partner(z, tensors - 1 - step) if linked else step

    def fetch(n, group):
        t, slot = tensor_at(chunk(n)[1]), rem(n, 2)
        pairs = (
            [(qkv_back_in, mixed_acts), (attended_in, attended_acts)],
            [(hidden_back_in, acts)],
            [(down_grads, staged)],
        )[group]
        return [
            pltpu.make_async_copy(src.at[t], dst.at[rem(n, dst.shape[0])], act_sem.at[slot, at])
            for at, (src, dst) in enumerate(pairs)
        ]

    def start(copies):
        for copy in copies:
            copy.start()

    pairs = ((normed_in, normed_t), (back_in, back_t), (two_in, two_t))
    loads = [pltpu.make_async_copy(src, flat.at[at], in_sem.at[at]) for at, (src, _) in enumerate(pairs)]
    start(loads)
    start(fetch(0, 0))

    if linked:
        chip, core, _, x_chip, y_chip, far_chip = position()
        x_dev, y_dev, other = (x_chip * 2 + core, z), (y_chip * 2 + core, z), (chip * 2 + 1 - core, z)
        half = pair.shape[2] // 2
        greet()
        shared = Share(packed, tokens_grad, *share_sems)
        shared.start()
        far = Far(tokens, weights, gains, biases, far_out, *far_scratch)
        far.start()

        def link(n, kind):
            sems = (send.at[n, kind], recv.at[n, kind])
            if kind == 0:
                return remote(staged.at[rem(n, 4), :, 1 - core], pair.at[n], *sems, other)
            if kind == 1:
                return remote(pair.at[n, far_chip, pl.ds(0, half)], x_half.at[n], *sems, x_dev)
            if kind == 2:
                return remote(pair.at[n, far_chip, pl.ds(half, half)], y_half.at[n], *sems, y_dev)
            if kind == 3:
                return remote(pair.at[n, x_chip], x_full.at[n], *sems, x_dev)
            return remote(pair.at[n, y_chip], y_full.at[n], *sems, y_dev)

        inner = rem(z, 2) + div(z, 2) == 1

        def z_link(n, kind):
            step = chunk(n)[1]
            step_there = step + 1 - 2 * rem(step, 2) if kind == 5 else tensors - 1 - step
            there = n + (step_there - step) * (1 + div(n + 4, 8))
            to = (chip * 2 + core, z_partner(z, 1 if kind == 5 else 3))
            return remote(
                pair.at[n, chip], z_sum.at[kind - 5, there], send.at[n, kind], recv.at[there, kind], to
            )

        def z_wait(n, kind):
            spot = z_sum.at[kind - 5, n]
            remote(spot, spot, send.at[n, kind], recv.at[n, kind], other).wait_recv()

        def add(ref, value):
            ref[...] = ref[...] + value

        def first(n):
            link(n, 0).wait_recv()
            link(n, 0).wait_send()
            slot = rem(n, 4)
            add(pair.at[n, far_chip], staged[slot, far_chip, core])
            link(n, 1).start()
            link(n, 2).start()
            for where in (x_chip, y_chip, chip):
                add(pair.at[n, where], staged[slot, where, core])

        def second(n):
            link(n, 1).wait_recv()
            add(pair.at[n, y_chip, pl.ds(0, half)], x_half[n])
            link(n, 4).start()
            link(n, 2).wait_recv()
            add(pair.at[n, x_chip, pl.ds(half, half)], y_half[n])
            link(n, 3).start()

        def third(n):
            link(n, 3).wait_recv()
            link(n, 4).wait_recv()
            mine = pair.at[n, chip]
            total = mine[...].astype(WIDE) + x_full[n].astype(WIDE) + y_full[n].astype(WIDE)
            mine[...] = total.astype(LOW)

            @pl.when(jnp.logical_and(chunk(n)[1] < tensors - 1, jnp.logical_not(inner)))
            def _():
                z_link(n, 5).start()

        def fourth(n):
            step = chunk(n)[1]

            @pl.when(jnp.logical_and(inner, step < 2))
            def _():
                z_wait(n, 5)
                add(pair.at[n, chip], z_sum[0, n])
                z_link(n, 6).start()

            @pl.when(jnp.logical_and(inner, step == 2))
            def _():
                z_wait(n, 6)
                add(pair.at[n, chip], z_sum[1, n])
                z_link(n, 5).start()

        def vec_link(step, kind):
            sems = (vec_send.at[step, kind], vec_recv.at[step, kind])
            t = z_partner(z, step)
            if kind == 0:
                return remote(vec_grads.at[t, :, 1 - core], vec_pair.at[step], *sems, other)
            if kind == 1:
                return remote(vec_pair.at[step, far_chip], vec_x.at[0, step], *sems, x_dev)
            if kind == 3:
                return remote(vec_pair.at[step, x_chip], vec_x.at[1, step], *sems, x_dev)
            if kind == 4:
                return remote(vec_pair.at[step, y_chip], vec_y.at[step], *sems, y_dev)
            return remote(vec_pair.at[step, chip], vec_z.at[step], *sems, (chip * 2 + core, t))

        steps = range(4)
        for step in steps:
            vec_link(step, 0).start()

        def vec_stage(stage):
            for step in steps:
                if stage == 0:
                    vec_link(step, 0).wait_recv()
                    vec_pair[step] += vec_grads[z_partner(z, step), :, core]
                    vec_link(step, 1).start()
                if stage == 1:
                    vec_link(step, 1).wait_recv()
                    add(vec_pair.at[step, y_chip], vec_x[0, step])
                    vec_link(step, 4).start()
                    vec_link(step, 3).start()
                if stage == 2:
                    vec_link(step, 3).wait_recv()
                    vec_link(step, 4).wait_recv()
                    add(vec_pair.at[step, chip], vec_x[1, step] + vec_y[step])
                    if step:
                        vec_link(step, 5).start()
                if stage == 3 and step:
                    vec_link(step, 5).wait_recv()
            if stage == 3:
                mine = vec_pair.at[0, chip]
                vec_out[...] = mine[...] + vec_z[1] + vec_z[2] + vec_z[3]
                for step in steps:
                    for kind in (0, 1, 3, 4, 5):
                        if kind < 5 or step:
                            vec_link(step, kind).wait_send()

    for load, (_, dst), at in zip(loads, pairs, range(3)):
        load.wait()
        dst[...] = flat[at].T
        if linked:
            vec_stage(at)

    def keep(n):
        group, step = chunk(n)
        return pltpu.make_async_copy(staged.at[rem(n, 4)], total_out.at[group, step], keep_sem.at[rem(n, 2)])

    def clear(n):
        if not linked:

            @pl.when(n > 1)
            def _():
                keep(n - 2).wait()

    shape = staged.shape[1:-1]

    @pl.loop(0, chunks + 6 if linked else chunks)
    def _(n):
        slot, place = rem(n, 2), rem(n, 4)
        paired = jnp.logical_and(n >= tensors, n < chunks)
        clear(n)

        @pl.when(n < tensors)
        def _():
            @pl.when(n + 1 < tensors)
            def _():
                start(fetch(n + 1, 0))

            @pl.when(n + 1 == tensors)
            def _():
                start(fetch(n + 1, 1))

            for copy in fetch(n, 0):
                copy.wait()
            wide = dot(normed_t[...], mixed_acts[slot]).astype(LOW)
            staged[place, :, :, :, : 3 * width] = wide.reshape(shape + (3 * width,))
            out = dot(back_t[...], attended_acts[slot]).astype(LOW)
            staged[place, :, :, :, 3 * width :] = out.reshape(shape + (width,))

        @pl.when(jnp.logical_and(paired, slot == 0))
        def _():
            start(fetch(n + 1, 2))
            for copy in fetch(n, 1):
                copy.wait()
            staged[place] = dot(two_t[...], acts[slot]).astype(LOW).reshape(shape + (hidden_width,))

        @pl.when(jnp.logical_and(paired, slot == 1))
        def _():
            @pl.when(n + 1 < chunks)
            def _():
                start(fetch(n + 1, 1))

            for copy in fetch(n, 2):
                copy.wait()

        if not linked:
            keep(n).start()
            return

        @pl.when(n < chunks)
        def _():
            link(n, 0).start()

        far.step(n - 1)
        for stage, lag in ((first, 1), (second, 2), (third, 3), (fourth, 6)):

            @pl.when(jnp.logical_and(n >= lag, n < chunks + lag))
            def _():
                stage(n - lag)

        for stage, step in enumerate((1, 3, 5, 7)):

            @pl.when(n == step)
            def _():
                shared.pass_on(stage)

    if linked:
        vec_stage(3)
        for group in range(3):
            n = max(n for n in range(chunks) if chunk(n)[0] == group)
            z_wait(n, 5)
            total_out[group] = pair[n, chip].astype(WIDE) + z_sum[0, n].astype(WIDE)

            @pl.when(inner)
            def _():
                z_wait(n, 6)
                total_out[group] += z_sum[1, n].astype(WIDE)

        @pl.loop(0, chunks)
        def _(n):
            for kind in range(1, 5):
                link(n, kind).wait_send()
            step = chunk(n)[1]

            @pl.when(jnp.logical_or(jnp.logical_and(step < tensors - 1, jnp.logical_not(inner)), jnp.logical_and(step == 2, inner)))
            def _():
                z_link(n, 5).wait_send()

            @pl.when(jnp.logical_and(step < 2, inner))
            def _():
                z_link(n, 6).wait_send()

        far.wait()
        shared.finish()
    else:
        keep(chunks - 2).wait()
        keep(chunks - 1).wait()


def weight_grads(
    packed, vec_grads, normed, two, back_low, qkv_back, attended, hidden_back, down_grads,
    tokens, weights, gains, biases, places, linked,
):
    tensors, rows, hidden_width = hidden_back.shape
    model = normed.shape[1]
    width = hidden_width // 4
    chunks = 3 * tensors
    dma = pltpu.SemaphoreType.DMA
    if linked:
        slab, chips = model // places, places // 2
        blocks = (chips, 2, slab, hidden_width)
        total = (3, slab, hidden_width), WIDE
        whole = (tensors,) + packed.shape
        vec_out = (8, 128)
        landing = [
            pltpu.VMEM((chunks, chips, slab, hidden_width), LOW),
            pltpu.VMEM((chunks, slab // 2, hidden_width), LOW),
            pltpu.VMEM((chunks, slab // 2, hidden_width), LOW),
            pltpu.VMEM((chunks, slab, hidden_width), LOW),
            pltpu.VMEM((chunks, slab, hidden_width), LOW),
            pltpu.VMEM((2, chunks, slab, hidden_width), LOW),
            pltpu.VMEM((4, chips, 8, 128), WIDE),
            pltpu.VMEM((2, 4, 8, 128), WIDE),
            pltpu.VMEM((4, 8, 128), WIDE),
            pltpu.VMEM((4, 8, 128), WIDE),
        ]
        vec_grads = vec_grads.reshape(tensors, chips, 2, 8, 128)
    else:
        blocks = (1, 1, model, hidden_width)
        total = (3, tensors) + blocks, LOW
        whole = vec_out = (8, 128)
        landing = [pltpu.VMEM((8, 128), WIDE)] * 10
    far_scratch = []
    if linked:
        padded = round_up(SEQ, ROWS)
        images = rows // padded - FAR_SENT
        far_rows, far_packed = images * padded, (round_up(images * SEQ, ROWS), model)
        far_scratch = [
            pltpu.VMEM((2,) + weights.shape[2:], LOW),
            pltpu.VMEM((images, padded + ROWS, model), LOW),
            pltpu.VMEM((far_rows, model), LOW),
            pltpu.VMEM((far_rows, model), LOW),
            pltpu.VMEM((far_rows, 3 * width), LOW),
            pltpu.VMEM((far_rows, width), LOW),
            pltpu.VMEM((far_rows, model), WIDE),
            pltpu.VMEM((far_rows, model), LOW),
            pltpu.VMEM((far_rows, hidden_width), WIDE),
            pltpu.VMEM((far_rows, hidden_width), LOW),
            pltpu.VMEM(far_packed, LOW),
            pltpu.VMEM((padded, padded), WIDE),
            pltpu.VMEM((padded, padded), LOW),
            pltpu.VMEM((images, 2, width, padded), LOW),
            dma((2,)),
            dma((images,)),
            dma,
        ]
    outs = ((whole, LOW), total, (vec_out, WIDE), (far_packed if linked else (8, 128), LOW))
    return pl.pallas_call(
        partial(grads_kernel, linked=linked),
        out_shape=[jax.ShapeDtypeStruct(shape, dtype) for shape, dtype in outs],
        in_specs=[ANY, VMEM] + [ANY] * 9 + [VMEM] * 2,
        out_specs=[ANY, VMEM if linked else ANY, VMEM, ANY],
        scratch_shapes=[pltpu.VMEM((3, rows, model), LOW)]
        + [pltpu.VMEM((model, rows), LOW)] * 3
        + [
            pltpu.VMEM((2, rows, hidden_width), LOW),
            pltpu.VMEM((2, rows, 3 * width), LOW),
            pltpu.VMEM((2, rows, width), LOW),
            pltpu.VMEM((4,) + blocks, LOW),
        ]
        + landing
        + [
            dma((3,)),
            dma((2, 2)),
            dma((2,)),
            dma((4, 6)),
            dma((4, 6)),
            dma((chunks, 7)),
            dma((chunks, 7)),
        ]
        + (share_scratch() if linked else [])
        + far_scratch,
        compiler_params=pltpu.CompilerParams(
            vmem_limit_bytes=58 * MEGA, has_side_effects=True, **({"collective_id": 2} if linked else {})
        ),
        name="weight_grads",
    )(
        packed, vec_grads, normed, two, back_low, qkv_back, attended, hidden_back, down_grads,
        tokens, weights, gains, biases,
    )


def adam_step(weight, gradient, first, second, rate, decay):
    first = BETA_ONE * first + (1.0 - BETA_ONE) * gradient
    second = BETA_TWO * second + (1.0 - BETA_TWO) * gradient * gradient
    corr_one = 1.0 - BETA_ONE**STEP
    corr_two = 1.0 - BETA_TWO**STEP
    updated = weight * (1.0 - rate * decay) - rate * (first / corr_one) / (
        jnp.sqrt(second / corr_two) + EPS_ADAM
    )
    return (first, second, updated)


def finish_kernel(*refs, linked, tensors, rows, slab, groups):
    refs = list(refs)
    wholes = [refs.pop(0) for _ in range(3)] if linked else []
    total, vec = refs.pop(0), refs.pop(0)
    inputs = [refs.pop(0) for _ in range(18)]
    flats = [refs.pop(0) for _ in range(2)] if linked else []
    outputs = [refs.pop(0) for _ in range(18)]
    held = [refs.pop(0) for _ in range(18)]
    news = [refs.pop(0) for _ in range(18)]
    small_in, small_out = refs.pop(0), refs.pop(0)
    params, moments = held[:6], held[6:]
    fetches = [pltpu.make_async_copy(inputs[at], held[at], small_in.at[at]) for at in range(18)]
    if linked:
        landed, far_landed, done, in_sem, out_sem, far_sem = refs

        far = far_block(lax.axis_index("tensor"), tensors)

        sent, far_rows = FAR_SENT * SEQ, rows - FAR_SENT * SEQ
        far_load = pltpu.make_async_copy(wholes[2], far_landed, far_sem)

        def load(at, t):
            return pltpu.make_async_copy(wholes[at].at[t], landed.at[at, t], in_sem.at[at, t])

        def store(at, t):
            begin, end = t * rows // ROWS * ROWS, (t + 1) * rows // ROWS * ROWS
            if t == tensors - 1:
                end = tensors * rows
            spot = pl.ds(begin, end - begin)
            return pltpu.make_async_copy(done.at[at, spot], flats[at].at[spot], out_sem.at[at, t])

        parts = [(at, t) for at in range(2) for t in range(tensors)]
        far_load.start()
        for part in parts:
            load(*part).start()
        for copy in fetches:
            copy.start()
        far_load.wait()
        for at, t in parts:
            load(at, t).wait()
            done[at, t * rows : (t + 1) * rows, :] = landed[at, t, :rows, :]
            if at == 0 and t in (0, tensors - 1):

                @pl.when(far == t)
                def _():
                    done[at, t * rows + sent : (t + 1) * rows, :] = far_landed[:far_rows, :]

            store(at, t).start()

    else:
        for copy in fetches:
            copy.start()

    width = total.shape[2] // 4

    for copy in fetches:
        copy.wait()

    def step(at, gradient, rate, decay, pick=()):
        weight, first, second = params[at], moments[2 * at], moments[2 * at + 1]
        values = adam_step(weight[pick], gradient, first[pick], second[pick], rate, decay)
        for out, value in zip(news[3 * at : 3 * at + 3], values):
            out[pick] = value

    for at in range(3):
        step(0, total[0, :, at * width : (at + 1) * width], RATE_MATRIX, DECAY_MATRIX, (at,))
    every = (slice(None),)
    step(1, total[0, :, 3 * width :].T, RATE_MATRIX, DECAY_MATRIX, every)
    step(2, total[1], RATE_MATRIX, DECAY_MATRIX, every)
    step(3, total[2], RATE_MATRIX, DECAY_MATRIX, every)
    step(4, vec[:6, :slab], RATE_VECTOR, 0.0, every)
    columns = vec[...].T
    shape = (columns.shape[0], 6 * groups)
    lane, row = (lax.broadcasted_iota(jnp.int32, shape, dim) for dim in (1, 0))
    attention = jnp.where(row < groups, 6 * row, jnp.where(row < 2 * groups, 6 * (row - groups) + 1, -1))
    hidden = jnp.where(row < 4 * groups, 6 * div(row, 4) + 2 + rem(row, 4), -1)
    picked = jnp.where(lane == attention, columns[:, 6:7], 0.0) + jnp.where(
        lane == hidden, columns[:, 7:8], 0.0
    )
    step(5, jnp.sum(picked, axis=0, keepdims=True), RATE_VECTOR, 0.0, every)
    stores = [pltpu.make_async_copy(news[at], outputs[at], small_out.at[at]) for at in range(18)]
    for copy in stores:
        copy.start()
    if linked:
        for part in parts:
            store(*part).wait()
    for copy in stores:
        copy.wait()


def finish(wholes, total, vec, params, moments, tensors, rows, slab, groups, linked):
    small = params + moments
    scratch = [pltpu.VMEM(value.shape, WIDE) for value in small]
    scratch += [pltpu.VMEM(param.shape, WIDE) for param in params for _ in range(3)]
    scratch += [pltpu.SemaphoreType.DMA((18,))] * 2
    outs, passed = [], ()
    if linked:
        passed = wholes
        model = wholes[0].shape[2]
        scratch += [
            pltpu.VMEM((2,) + wholes[0].shape, LOW),
            pltpu.VMEM(wholes[2].shape, LOW),
            pltpu.VMEM((2, tensors * rows, model), LOW),
            pltpu.SemaphoreType.DMA((2, tensors)),
            pltpu.SemaphoreType.DMA((2, tensors)),
            pltpu.SemaphoreType.DMA,
        ]
        outs = [jax.ShapeDtypeStruct((tensors * rows, model), LOW)] * 2
    news = [jax.ShapeDtypeStruct(param.shape, WIDE) for param in params for _ in range(3)]
    results = pl.pallas_call(
        partial(finish_kernel, linked=linked, tensors=tensors, rows=rows, slab=slab, groups=groups),
        out_shape=outs + news,
        in_specs=[ANY] * len(passed) + [VMEM] * 2 + [ANY] * 18,
        out_specs=[ANY] * (len(outs) + 18),
        scratch_shapes=scratch,
        compiler_params=pltpu.CompilerParams(vmem_limit_bytes=58 * MEGA),
        name="finish",
    )(*passed, total, vec, *small)
    if linked:
        return results[:2], list(results[2:])
    return wholes, list(results)


def own_parts(params, slab, width):
    qkv, out, up, down_t, shared, split = params
    mixed = jnp.concatenate([qkv[0], qkv[1], qkv[2], out.T], axis=1)
    table = split.reshape(-1, 6)
    rows = [shared, jnp.concatenate([table[:, 0], table[:, 1]])[None], table[:, 2:].reshape(1, -1)]
    vec = jnp.concatenate([jnp.pad(row, ((0, 0), (0, 128 - row.shape[1]))) for row in rows])
    return jnp.stack([mixed, up, down_t]).astype(LOW), vec


def per_device(
    tokens,
    cotangent,
    qkv_weight,
    out_weight,
    up_weight,
    down_weight,
    shared_vectors,
    split_vectors,
    qkv_first,
    qkv_second,
    out_first,
    out_second,
    up_first,
    up_second,
    down_first,
    down_second,
    shared_first,
    shared_second,
    split_first,
    split_second,
    *,
    places,
    tensors,
):
    linked = places == 8 and tensors == 4
    slab, width = qkv_weight.shape[1], qkv_weight.shape[2]
    model = slab * places
    groups = width // places
    rows = tokens.shape[0] // tensors
    images = rows // SEQ

    params = (qkv_weight, out_weight, up_weight, down_weight.T, shared_vectors, split_vectors)
    moments = (
        qkv_first, qkv_second, out_first, out_second, up_first, up_second,
        down_first.T, down_second.T, shared_first, shared_second, split_first, split_second,
    )
    sources = params
    if not linked:
        shard, vec = own_parts(params, slab, width)
        shard = lax.all_gather(lax.all_gather(shard, "dp", axis=1, tiled=True), "tensor", axis=1)
        vec = lax.all_gather(lax.all_gather(vec, "dp"), "tensor")
        sources = (shard, vec.reshape(tensors, places // 2, 2, 8, 128))
    packed, weights, own, back, back_t, gains, biases, *kept = forward(
        tokens, cotangent, sources, images, width, tensors, places, linked
    )
    normed, qkv, probs, attended, middle, two, hidden, slope = kept
    if not linked:
        weights = shard.reshape(3, tensors, 1, 1, model, 4 * width)
    packed_grad, block_out, hidden_back, back_low, qkv_back, vec_grads, down_grads = chain(
        packed, own, back, back_t, gains, weights, qkv, probs, middle, slope, hidden, places, linked
    )
    tokens_grad, total, vec_total, far = weight_grads(
        packed_grad, vec_grads, normed, two, back_low, qkv_back, attended, hidden_back, down_grads,
        tokens, weights, gains, biases, places, linked,
    )
    if linked:
        shares = (block_out, tokens_grad, far)
    else:
        shares = [lax.all_gather(part[:rows], "tensor", axis=0, tiled=True) for part in (packed, packed_grad)]
        total = total.reshape(3, tensors, model, 4 * width)
        total = lax.psum_scatter(total, "dp", scatter_dimension=2, tiled=True)
        total = lax.psum_scatter(total, "tensor", scatter_dimension=1).astype(WIDE)
        vec_total = lax.psum_scatter(vec_grads, "dp", scatter_dimension=1)
        vec_total = lax.psum_scatter(vec_total, "tensor", scatter_dimension=0)
    shares, news = finish(shares, total, vec_total, params, moments, tensors, rows, slab, groups, linked)
    news[9:12] = [new.T for new in news[9:12]]
    return (*shares, *news)


def solution(mesh):
    qkv, rows, cols = P(None, "dp", "tensor"), P("tensor", "dp"), P("dp", "tensor")
    shared, images = P(None, "dp"), P("dp", None)
    params = (qkv, rows, cols, rows, shared, rows)
    moments = tuple(spec for spec in params for _ in range(2))
    results = tuple(spec for spec in params for _ in range(3))
    return jax.shard_map(
        partial(per_device, places=mesh.shape["dp"], tensors=mesh.shape["tensor"]),
        mesh=mesh,
        in_specs=(images, images) + params + moments,
        out_specs=(images, images) + results,
        check_vma=False,
    )
```

```python
import math
from functools import partial

import jax
import jax.numpy as jnp
from jax import lax
from jax.experimental import pallas as pl
from jax.experimental.pallas import tpu as pltpu
from jax.sharding import PartitionSpec as P

HEAD = 64
SEQ = 197
STEP = 10

EPS_NORM = 1e-06
EPS_ADAM = 1e-08
BETA_ONE = 0.9
BETA_TWO = 0.999
RATE_MATRIX = 0.05
RATE_VECTOR = 0.2
DECAY_MATRIX = 0.05

LOW = jnp.bfloat16
WIDE = jnp.float32
MESH = pl.DeviceIdType.MESH
ROWS = 16
BLOCK = 64
STRIP = 32
FAR_STEP = 64
FAR_SENT = 0
MEGA = 1024 * 1024
VMEM = pl.BlockSpec(memory_space=pltpu.VMEM)
ANY = pl.BlockSpec(memory_space=pl.ANY)


def round_up(value, unit):
    return -(-value // unit) * unit


def rem(left, right):
    return left % right if isinstance(left, int) else lax.rem(left, right)


def div(left, right):
    return left // right if isinstance(left, int) else lax.div(left, right)


def position():
    place, z = lax.axis_index("dp"), lax.axis_index("tensor")
    core, chip = rem(place, 2), div(place, 2)
    x, y = rem(chip, 2), div(chip, 2)
    return chip, core, z, y * 2 + (1 - x), (1 - y) * 2 + x, (1 - y) * 2 + (1 - x)


def z_partner(z, step):
    return z + rem(step, 2) * (1 - 2 * rem(z, 2)) + div(step, 2) * (2 - 4 * div(z, 2))


def chunk(n):
    late = div(n + 4, 8)
    return late * (1 + rem(n, 2)), (1 - late) * n + late * div(n - 4, 2)


def greet(wait=True):
    chip, core, z, x_chip, y_chip, _ = position()
    barrier = pltpu.get_barrier_semaphore()
    targets = [(x_chip * 2 + core, z), (y_chip * 2 + core, z), (chip * 2 + 1 - core, z)]
    targets += [(chip * 2 + core, z_partner(z, step)) for step in (1, 2, 3)]
    for target in targets:
        pl.semaphore_signal(barrier, inc=1, device_id=target, device_id_type=MESH)
    if wait:
        pl.semaphore_wait(barrier, len(targets))
    return barrier, len(targets)


def remote(src, dst, send, recv, target):
    return pltpu.make_async_remote_copy(
        src_ref=src, dst_ref=dst, send_sem=send, recv_sem=recv, device_id=target, device_id_type=MESH
    )


class Share:
    pieces = 2

    def __init__(self, part, whole, send, recv, own, far=range(pieces), far_size=None):
        self.far, self.far_size = far, far_size
        chip, core, self.z, _, _, _ = position()
        self.part, self.whole, self.send, self.recv = part, whole, send, recv
        self.here = chip * 2 + core
        self.size = part.shape[0] // self.pieces
        self.own = pltpu.make_async_copy(part, whole.at[self.z], own)
        self.inner = rem(self.z, 2) + div(self.z, 2) == 1

    def copy(self, kind, piece):
        z = self.z
        short = kind in (2, 4) and self.far_size
        rows = pl.ds(piece * self.size, self.far_size if short else self.size)
        block = z_partner(z, (0, 0, 1, 3, 2)[kind])
        src = (self.part if kind < 2 else self.whole.at[block]).at[rows]
        target = z_partner(z, (1, 3, 3, 1, 1)[kind])
        lane = (0, 1, 2, 1, 2)[kind]
        return remote(
            src, self.whole.at[block, rows], self.send.at[kind, piece], self.recv.at[lane, piece],
            (self.here, target),
        )

    def start(self):
        self.own.start()
        for piece in range(self.pieces):
            self.copy(0, piece).start()

        @pl.when(self.inner)
        def _():
            for piece in range(self.pieces):
                self.copy(1, piece).start()

    def pass_on(self, stage):
        near, piece = stage < self.pieces, stage % self.pieces

        @pl.when(self.inner)
        def _():
            if near:
                self.copy(0, piece).wait_recv()
                if piece in self.far:
                    self.copy(2, piece).start()
                self.copy(1, piece).wait_recv()
                self.copy(3, piece).start()
            elif piece in self.far:
                self.copy(2, piece).wait_recv()
                self.copy(4, piece).start()

    def finish(self):
        def each(kinds):
            for kind in kinds:
                for piece in self.far if kind in (2, 4) else range(self.pieces):
                    yield self.copy(kind, piece)

        @pl.when(jnp.logical_not(self.inner))
        def _():
            for copy in each((0, 3, 4)):
                copy.wait_recv()
            for copy in each((0,)):
                copy.wait_send()

        @pl.when(self.inner)
        def _():
            for copy in each(range(5)):
                copy.wait_send()

        self.own.wait()


def share_scratch():
    return [
        pltpu.SemaphoreType.DMA((5, Share.pieces)),
        pltpu.SemaphoreType.DMA((3, Share.pieces)),
        pltpu.SemaphoreType.DMA,
    ]


def dot(left, right, left_dim=1, right_dim=0):
    return lax.dot_general(
        left, right, (((left_dim,), (right_dim,)), ((), ())), preferred_element_type=WIDE
    )


def fill_unit(unit):
    row, column = (lax.broadcasted_iota(jnp.int32, unit.shape, dim) for dim in (0, 1))
    unit[...] = jnp.where(row == column, 1.0, 0.0).astype(LOW)


def flip(value, unit):
    count = value.shape[1]
    return dot(unit[:count, :count], value, 1, 1).astype(LOW)


def block_at(at):
    return pl.ds(pl.multiple_of(at * BLOCK, BLOCK), BLOCK)


def norm_parts(values):
    centre = values - jnp.mean(values, axis=-1, keepdims=True)
    factor = lax.rsqrt(jnp.mean(centre * centre, axis=-1, keepdims=True) + EPS_NORM)
    return centre * factor, factor


def norm_backward(grad_out, unit, factor, gain):
    scaled = grad_out * gain
    return factor * (
        scaled
        - jnp.mean(scaled, axis=-1, keepdims=True)
        - unit * jnp.mean(scaled * unit, axis=-1, keepdims=True)
    )


def fold(values):
    return jnp.sum(values.reshape(values.shape[0] // 8, 8, values.shape[1]), axis=0)


def attend(image, qkv, attended, mask, unit, turn, kept=None):
    padded, width = mask.shape[0], attended.shape[1]
    scale = 1.0 / math.sqrt(HEAD)
    spot = pl.ds(pl.multiple_of(image * padded, padded), padded)
    turn[0] = flip(qkv[spot, 2 * width : 3 * width], unit)
    for head in range(width // HEAD):
        lanes = head * HEAD
        query = qkv[spot, lanes : lanes + HEAD]
        key = qkv[spot, width + lanes : width + lanes + HEAD]
        scores = dot(key, query, 1, 1) + mask[...]
        highest = jnp.max(scores, axis=0, keepdims=True)
        exponent = jnp.exp((scores - highest) * scale)
        total = jnp.sum(exponent, axis=0, keepdims=True)
        prob = (exponent * (1.0 / total)).astype(LOW)
        if kept is not None:
            kept[image, head] = prob
        turn[1, lanes : lanes + HEAD, :] = dot(turn[0, lanes : lanes + HEAD, :], prob).astype(LOW)
    attended[spot, :] = flip(turn[1], unit)


def fill_mask(mask):
    mask[...] = jnp.where(lax.broadcasted_iota(jnp.int32, mask.shape, 0) < SEQ, 0.0, -1e30)


def gelu_parts(value):
    cdf = 0.5 * (1.0 + lax.erf(value * (1.0 / math.sqrt(2.0))))
    return cdf, jnp.exp(-0.5 * value * value) * (1.0 / math.sqrt(2.0 * math.pi))


class Rows:
    def __init__(self, src, window, sems, begin, images, padded):
        self.src, self.window, self.sems = src, window, sems
        self.begin, self.images, self.padded = begin, images, padded

    def copy(self, image):
        begin = (self.begin + image) * SEQ
        last = self.src.shape[0] - SEQ
        aligned = div(begin, ROWS) * ROWS - ROWS * div(begin, last)
        rows = pl.ds(pl.multiple_of(aligned, ROWS), self.window.shape[1])
        copy = pltpu.make_async_copy(self.src.at[rows], self.window.at[image], self.sems.at[image])
        return copy, begin - aligned

    def fetch(self):
        for image in range(self.images):
            self.copy(image)[0].start()

    def place(self, dst):
        span, padded = self.window.shape[1], self.padded

        @pl.loop(0, self.images)
        def _(image):
            copy, shift = self.copy(image)
            copy.wait()
            moved = pltpu.roll(self.window[image].astype(WIDE), rem(span - shift, span), axis=0)[:padded]
            inside = lax.broadcasted_iota(jnp.int32, (padded, 1), 0) < SEQ
            spot = pl.ds(pl.multiple_of(image * padded, padded), padded)
            dst[spot, :] = jnp.where(inside, moved, 0.0).astype(LOW)


def far_block(z, tensors):
    return (tensors - 1) * (1 - div(z, tensors // 2))


def pack_images(values, work, images, padded):
    for image in range(images):
        work[image * SEQ : (image + 1) * SEQ, :] = values[image * padded : image * padded + SEQ, :]


def arrange(raw, shard, vec, slab, width):
    qkv, out, up, down_t, shared, split = raw
    for at in range(3):
        shard[0, :, at * width : (at + 1) * width] = qkv[at].astype(LOW)
    shard[0, :, 3 * width :] = out[...].T.astype(LOW)
    shard[1] = up[...].astype(LOW)
    shard[2] = down_t[...].astype(LOW)
    vec[...] = jnp.zeros_like(vec)
    vec[:6, :slab] = shared[...]
    count = split.shape[1]
    groups = count // 6
    column = jnp.broadcast_to(split[...], (8, count)).T[:, :1]
    row, lane = (lax.broadcasted_iota(jnp.int32, (count, 128), dim) for dim in (0, 1))
    attention = jnp.where(lane < groups, 6 * lane, jnp.where(lane < 2 * groups, 6 * (lane - groups) + 1, -1))
    hidden = jnp.where(lane < 4 * groups, 6 * div(lane, 4) + 2 + rem(lane, 4), -1)
    for at, wanted in ((6, attention), (7, hidden)):
        vec[at : at + 1, :] = jnp.sum(jnp.where(row == wanted, column, 0.0), axis=0, keepdims=True)


def forward_kernel(
    tokens, cotangent, *refs, linked,
):
    count = 6 if linked else 2
    forward_body(tokens, cotangent, refs[:count], *refs[count:], linked=linked)


def forward_body(
    tokens, cotangent, sources,
    packed, weights_out, own_out, back_out, back_t_out, gains_out, biases_out,
    normed_out, qkv_out, probs_out, attended_out, middle_out, two_out, hidden_out, slope_out,
    held, vec_held, gains, biases, window, own, back, back_t,
    normed, qkv, probs, attended, middle, two, hidden, slope, work, feed,
    mask, unit, turn, in_sem, row_sem, out_sem, act_sem, weight_sem, vec_send, vec_recv, send, recv, *own_parts,
    linked,
):
    tensors = held.shape[1]
    model, hidden_width = own.shape[1], held.shape[-1]
    width = hidden_width // 4
    heads = width // HEAD
    images, padded = probs.shape[1], probs.shape[-1]
    rows = images * padded
    scale = 1.0 / math.sqrt(HEAD)
    chunks = 3 * tensors
    z = lax.axis_index("tensor")

    own_tokens = Rows(tokens, window, row_sem, z * images, images, padded)
    own_cotangent = Rows(cotangent, window, row_sem, z * images, images, padded)

    def fill_constants():
        fill_unit(unit)
        fill_mask(mask)
        biases[...] = jnp.zeros_like(biases)

    own_tokens.fetch()

    if linked:
        chip, core, _, x_chip, y_chip, far_chip = position()
        x_dev, y_dev, other = (x_chip * 2 + core, z), (y_chip * 2 + core, z), (chip * 2 + 1 - core, z)
        half = held.shape[4] // 2
        weights, vec, *raw = own_parts
        raw_copies = [
            pltpu.make_async_copy(src, dst, vec_send.at[div(at, 3), rem(at, 3)])
            for at, (src, dst) in enumerate(zip(sources, raw))
        ]
        for copy in raw_copies:
            copy.start()
        barrier = greet(wait=False)
        for copy in raw_copies:
            copy.wait()
        arrange(raw, weights, vec, held.shape[4], width)
        pl.semaphore_wait(*barrier)

        def link(n, kind):
            group, step = chunk(n)
            t = z_partner(z, step)
            sems = (send.at[n, kind], recv.at[n, kind])
            spot = held.at[group, t, chip, core]
            if kind == 0:
                to = (chip * 2 + core, t)
                return remote(weights.at[group], held.at[group, z, chip, core], *sems, to)
            if kind == 1:
                return remote(spot, spot, *sems, x_dev)
            if kind == 2:
                return remote(spot, spot, *sems, y_dev)
            if kind == 3:
                spot = held.at[group, t, x_chip, core, pl.ds(0, half)]
                return remote(spot, spot, *sems, y_dev)
            if kind == 4:
                spot = held.at[group, t, y_chip, core, pl.ds(half, half)]
                return remote(spot, spot, *sems, x_dev)
            spot = held.at[group, t, :, core]
            return remote(spot, spot, *sems, other)

        def vec_link(step, kind):
            t = z_partner(z, step)
            sems = (vec_send.at[step, kind], vec_recv.at[step, kind])
            if kind == 0:
                return remote(vec, vec_held.at[z, chip, core], *sems, (chip * 2 + core, t))
            spot = vec_held.at[t, x_chip if kind == 3 else chip, core]
            if kind == 5:
                spot = vec_held.at[t, :, core]
            return remote(spot, spot, *sems, {1: x_dev, 2: y_dev, 3: y_dev, 5: other}[kind])

        own_copies = [
            pltpu.make_async_copy(weights.at[group], held.at[group, z, chip, core], in_sem.at[group, 0])
            for group in range(3)
        ] + [pltpu.make_async_copy(vec, vec_held.at[z, chip, core], in_sem.at[3, 0])]
        for copy in own_copies:
            copy.start()
        for step in (1, 2, 3):
            vec_link(step, 0).start()
        for n in range(chunks):
            if chunk(n)[1]:
                link(n, 0).start()

        def first(n):
            if isinstance(n, int):
                if chunk(n)[1]:
                    link(n, 0).wait_recv()
            else:

                @pl.when(chunk(n)[1] > 0)
                def _():
                    link(n, 0).wait_recv()

            link(n, 1).start()
            link(n, 2).start()

        def second(n):
            link(n, 1).wait_recv()
            link(n, 3).start()
            link(n, 2).wait_recv()
            link(n, 4).start()

        def third(n):
            link(n, 3).wait_recv()
            link(n, 4).wait_recv()
            link(n, 5).start()

        def arrived(n):
            link(n, 5).wait_recv()

        def serve(n):
            first(n + 2)
            second(n)
            third(n - 2)

        for copy in own_copies:
            copy.wait()
        first(0)
        for step in range(4):
            if step:
                vec_link(step, 0).wait_recv()
            vec_link(step, 1).start()
            vec_link(step, 2).start()
        own_tokens.place(own)
        own_cotangent.fetch()
        first(1)
        for step in range(4):
            vec_link(step, 1).wait_recv()
            vec_link(step, 3).start()
        second(0)
        fill_constants()
        for step in range(4):
            vec_link(step, 2).wait_recv()
            vec_link(step, 3).wait_recv()
            vec_link(step, 5).start()
        third(0)
        first(2)
        own_cotangent.place(back)
        back_t[...] = back[...].T
        second(1)
        first(3)
        for step in range(4):
            vec_link(step, 5).wait_recv()
    else:
        weights, vec = sources

        def local(n):
            group, step = chunk(n)
            return pltpu.make_async_copy(
                weights.at[group, step], held.at[group, step, 0, 0], in_sem.at[group, step]
            )

        for n in range(chunks):
            local(n).start()
        copy = pltpu.make_async_copy(vec, vec_held, in_sem.at[3, 0])
        copy.start()
        copy.wait()

        def arrived(n):
            local(n).wait()

        own_tokens.place(own)
        own_cotangent.fetch()
        fill_constants()
        own_cotangent.place(back)
        back_t[...] = back[...].T

    def tensor_at(step):
        return z_partner(z, step) if linked else step

    def keep_weights(n):
        group, step = chunk(n)
        t = tensor_at(step)
        return pltpu.make_async_copy(held.at[group, t], weights_out.at[group, t], weight_sem.at[n])

    def ready(n):
        arrived(n)
        if linked:
            keep_weights(n).start()

    def save(at, src, dst):
        return pltpu.make_async_copy(src, dst, out_sem.at[at])

    places = vec_held.shape[1] * vec_held.shape[2]
    slab, share = model // places, width // places

    @pl.loop(0, tensors)
    def _(t):
        for place in range(places):
            piece = vec_held[t, place // 2, place % 2]
            gains[t, :, place * slab : (place + 1) * slab] = piece[:, :slab]
            biases[t, :, place * share : (place + 1) * share] = piece[:, :share]
            begin = 2 * width + place * share
            biases[t, :, begin : begin + share] = piece[:, share : 2 * share]

    saves = [save(8, own, own_out), save(9, gains, gains_out), save(10, back, back_out)]
    saves += [save(11, biases, biases_out), save(12, back_t, back_t_out)]
    for copy in saves:
        copy.start()

    @pl.loop(0, rows // BLOCK)
    def _(at):
        block = block_at(at)
        inputs = own[block, :].astype(WIDE)
        unit, _ = norm_parts(inputs)
        normed[block, :] = (unit * gains[0, 0:1, :] + gains[0, 1:2, :]).astype(LOW)
        middle[block, :] = inputs + gains[0, 4:5, :]

    saves.append(save(0, normed, normed_out))
    saves[-1].start()

    @pl.loop(0, tensors)
    def _(step):
        t = tensor_at(step)
        ready(step)
        wide = held[0, t, :, :, :, : 3 * width].reshape(model, 3 * width)
        qkv[t] = (dot(normed[...], wide) + biases[t, 6:7, :]).astype(LOW)

        @pl.loop(0, 2)
        def _(part):
            for at in range(images // 2):
                image = part * (images // 2) + at
                attend(image, qkv.at[t], attended.at[t], mask, unit, turn.at[at], probs.at[t])

            if linked:

                @pl.when(jnp.logical_and(part == 0, step == 0))
                def _():
                    first(4)
                    second(2)

                @pl.when(jnp.logical_and(part == 0, step == 1))
                def _():
                    serve(4)

                @pl.when(part == 1)
                def _():
                    serve(3 + step + div(step + 3, 4))

        out = held[0, t, :, :, :, 3 * width :].reshape(model, width)
        middle[...] += dot(attended[t], out, 1, 1)

    saves += [
        save(1, qkv, qkv_out),
        save(2, probs, probs_out),
        save(3, attended, attended_out),
        save(4, middle, middle_out),
    ]
    for copy in saves[-4:]:
        copy.start()

    @pl.loop(0, rows // BLOCK)
    def _(at):
        block = block_at(at)
        values = middle[block, :]
        unit, _ = norm_parts(values)
        two[block, :] = (unit * gains[0, 2:3, :] + gains[0, 3:4, :]).astype(LOW)
        feed[block, :] = values + gains[0, 5:6, :]

    saves.append(save(5, two, two_out))
    saves[-1].start()

    half_rows, wide_lanes = rows // 2, 256
    halves = [pl.ds(0, half_rows), pl.ds(half_rows, half_rows)]

    def keep_acts(step):
        t = tensor_at(step)
        return [
            pltpu.make_async_copy(src.at[t], dst.at[t], act_sem.at[at, step])
            for at, (src, dst) in enumerate(((hidden, hidden_out), (slope, slope_out)))
        ]

    def up_part(half, step, lanes):
        weight = held[1, tensor_at(step), :, :, :, lanes].reshape(model, wide_lanes)
        work[halves[half], lanes] = dot(two[halves[half], :], weight)

    def act_part(half, step, at):
        t = tensor_at(step)
        block = pl.ds(half * half_rows + at * STRIP, STRIP)
        value = work[block, :] + gains[t, 7:8, :]
        cdf, density = gelu_parts(value)
        hidden[t, block, :] = (value * cdf).astype(LOW)
        slope[t, block, :] = (cdf + value * density).astype(LOW)

    def down_part(half, step, lanes):
        t = tensor_at(step)
        weight = held[2, t].reshape(model, hidden_width)[lanes]
        feed[halves[half], lanes] += dot(hidden[t, halves[half], :], weight, 1, 1)

    def together(up=None, act=None, down=None):
        lanes = [slice(at, at + wide_lanes) for at in range(0, hidden_width, wide_lanes)]
        products = [partial(up_part, *up, lane) for lane in lanes] if up else []
        products += [partial(down_part, *down, lane) for lane in lanes] if down else []
        acts = [partial(act_part, *act, at) for at in range(half_rows // STRIP)] if act else []
        every = -(-len(acts) // max(len(products), 1))
        for at, product in enumerate(products):
            product()
            for part in acts[at * every : (at + 1) * every]:
                part()
        for part in acts[len(products) * every :]:
            part()

    ready(tensors)
    together(up=(0, 0))
    if linked:
        serve(8)
    together(up=(1, 0), act=(0, 0))
    if linked:
        serve(9)

    @pl.loop(1, tensors)
    def _(step):
        ready(2 * step + 3)
        ready(2 * step + 4)
        together(up=(0, step), act=(1, step - 1), down=(0, step - 1))
        for copy in keep_acts(step - 1):
            copy.start()
        if linked:

            @pl.when(step == 1)
            def _():
                second(10)
                third(8)

            @pl.when(step == 2)
            def _():
                third(10)

        together(up=(1, step), act=(0, step), down=(1, step - 1))
        if linked:

            @pl.when(step == 1)
            def _():
                second(11)
                third(9)

            @pl.when(step == 2)
            def _():
                third(11)

    last = tensors - 1
    ready(chunks - 1)
    together(act=(1, last), down=(0, last))
    for copy in keep_acts(last):
        copy.start()
    together(down=(1, last))
    for step in range(tensors):
        saves += keep_acts(step)
    pack_images(feed, work, images, padded)
    packed[...] = work[: packed.shape[0], :].astype(LOW)
    for copy in saves:
        copy.wait()
    if linked:
        for step in range(4):
            for kind in (0, 1, 2, 3, 5):
                if kind or step:
                    vec_link(step, kind).wait_send()

        @pl.loop(0, chunks)
        def _(n):
            @pl.when(chunk(n)[1] > 0)
            def _():
                link(n, 0).wait_send()

            for kind in range(1, 6):
                link(n, kind).wait_send()
            keep_weights(n).wait()


def forward(tokens, cotangent, sources, images, width, tensors, places, linked):
    model, hidden_width = tokens.shape[1], 4 * width
    padded, heads = round_up(SEQ, ROWS), width // HEAD
    rows, packed_rows = images * padded, round_up(images * SEQ, 2 * ROWS)
    if linked:
        blocks = (3, tensors, places // 2, 2, model // places, hidden_width)
    else:
        blocks = (3, tensors, 1, 1, model, hidden_width)
    kept = (
        ((rows, model), LOW),
        ((tensors, rows, 3 * width), LOW),
        ((tensors, images, heads, padded, padded), LOW),
        ((tensors, rows, width), LOW),
        ((rows, model), WIDE),
        ((rows, model), LOW),
        ((tensors, rows, hidden_width), LOW),
        ((tensors, rows, hidden_width), LOW),
    )
    outs = (
        ((packed_rows, model), LOW),
        (blocks if linked else (8, 128), LOW),
        ((rows, model), LOW),
        ((rows, model), LOW),
        ((model, rows), LOW),
        ((tensors, 8, model), WIDE),
        ((tensors, 8, 3 * width), WIDE),
    ) + kept
    dma = pltpu.SemaphoreType.DMA
    own_parts = []
    if linked:
        own_parts = [pltpu.VMEM((3, model // places, hidden_width), LOW), pltpu.VMEM((8, 128), WIDE)]
        own_parts += [pltpu.VMEM(source.shape, WIDE) for source in sources]
    return pl.pallas_call(
        partial(forward_kernel, linked=linked),
        out_shape=[jax.ShapeDtypeStruct(shape, dtype) for shape, dtype in outs],
        in_specs=[ANY] * (2 + len(sources)),
        out_specs=[VMEM] + [ANY] * (len(outs) - 1),
        scratch_shapes=[
            pltpu.VMEM(blocks, LOW),
            pltpu.VMEM((tensors, places // 2, 2, 8, 128), WIDE),
            pltpu.VMEM((tensors, 8, model), WIDE),
            pltpu.VMEM((tensors, 8, 3 * width), WIDE),
            pltpu.VMEM((images, padded + ROWS, model), LOW),
            pltpu.VMEM((rows, model), LOW),
            pltpu.VMEM((rows, model), LOW),
            pltpu.VMEM((model, rows), LOW),
        ]
        + [pltpu.VMEM(shape, dtype) for shape, dtype in kept]
        + [
            pltpu.VMEM((rows, hidden_width), WIDE),
            pltpu.VMEM((rows, model), WIDE),
            pltpu.VMEM((padded, padded), WIDE),
            pltpu.VMEM((padded, padded), LOW),
            pltpu.VMEM((images // 2, 2, width, padded), LOW),
            dma((4, tensors)),
            dma((images,)),
            dma((13,)),
            dma((2, tensors)),
            dma((3 * tensors,)),
            dma((4, 6)),
            dma((4, 6)),
            dma((3 * tensors, 6)),
            dma((3 * tensors, 6)),
        ]
        + own_parts,
        compiler_params=pltpu.CompilerParams(
            vmem_limit_bytes=58 * MEGA, has_side_effects=True, **({"collective_id": 0} if linked else {})
        ),
        name="forward",
    )(tokens, cotangent, *sources)


def chain_kernel(
    packed, tokens_in, cotangent, cot_t_in, gains, weights, qkv_in, probs_in, middle_in, slope_in, hidden_in,
    packed_grad, block_out, hidden_back_out, back_low_out, qkv_back_out, vec_grads, down_grads,
    tokens, cot_t, mixed, stream, slopes, acts, staged, qkv, probs, middle, work, total, back, back_low, hidden_back, attended_back,
    qkv_back, rows_eight, bias_rows, unit, turn, in_sem, stream_sem, out_sem, down_sem, *share_sems,
    linked,
):
    rows, model = cotangent.shape
    tensors, hidden_width = weights.shape[1], weights.shape[-1]
    width = hidden_width // 4
    heads = width // HEAD
    images, padded = probs.shape[1], probs.shape[-1]
    scale = 1.0 / math.sqrt(HEAD)
    places = vec_grads.shape[1]
    slab, part = model // places, width // places

    if linked:
        greet()
        shared = Share(packed, block_out, *share_sems, far=())
        shared.start()

    def fetch(t):
        slot = rem(t, 2)
        pairs = (
            (weights.at[2, t], stream.at[slot, 0]),
            (slope_in.at[t], slopes.at[slot]),
            (weights.at[1, t], stream.at[slot, 1]),
            (hidden_in.at[t], acts.at[slot]),
        )
        return [
            pltpu.make_async_copy(src, dst, stream_sem.at[slot, at]) for at, (src, dst) in enumerate(pairs)
        ]

    for copy in fetch(0):
        copy.start()
    turned = pltpu.make_async_copy(cot_t_in, cot_t, in_sem.at[5])
    turned.start()
    pairs = (
        (middle_in, middle), (weights.at[0], mixed), (qkv_in, qkv), (probs_in, probs), (tokens_in, tokens),
    )
    loads = [pltpu.make_async_copy(src, dst, in_sem.at[at]) for at, (src, dst) in enumerate(pairs)]
    for copy in loads:
        copy.start()
    total[...] = jnp.zeros_like(total)
    rows_eight[...] = jnp.zeros_like(rows_eight)
    fill_unit(unit)

    def keep_down(t):
        slot = rem(t, 2)
        return pltpu.make_async_copy(staged.at[slot], down_grads.at[t], down_sem.at[slot])

    def keep_hidden(t):
        slot = rem(t, 2)
        return pltpu.make_async_copy(hidden_back.at[slot], hidden_back_out.at[t], out_sem.at[slot])

    @pl.loop(0, tensors)
    def _(t):
        slot = rem(t, 2)

        @pl.when(t + 1 < tensors)
        def _():
            for copy in fetch(t + 1):
                copy.start()

        @pl.when(t > 1)
        def _():
            keep_hidden(t - 2).wait()
            keep_down(t - 2).wait()

        copies = fetch(t)
        copies[0].wait()
        work[...] = dot(cotangent[...], stream[slot, 0].reshape(model, hidden_width))
        copies[1].wait()

        def through(at, sums):
            block = block_at(at)
            low = (work[block, :] * slopes[slot, block, :].astype(WIDE)).astype(LOW)
            hidden_back[slot, block, :] = low
            return sums + fold(low.astype(WIDE))

        sums = lax.fori_loop(0, rows // BLOCK, through, jnp.zeros((8, hidden_width), WIDE))
        rows_eight[t, 7:8, :] = jnp.sum(sums, axis=0, keepdims=True)
        keep_hidden(t).start()
        copies[2].wait()
        total[...] += dot(hidden_back[slot], stream[slot, 1].reshape(model, hidden_width), 1, 1)
        copies[3].wait()

        @pl.when(t == 0)
        def _():
            turned.wait()

        staged[slot] = dot(cot_t[...], acts[slot]).astype(LOW).reshape(staged.shape[1:])
        keep_down(t).start()
        if linked:

            @pl.when(t == tensors // 2)
            def _():
                shared.pass_on(0)
    loads[0].wait()

    def second_norm(at, sums):
        block = block_at(at)
        unit, factor = norm_parts(middle[block, :])
        grad_out = total[block, :]
        from_above = cotangent[block, :].astype(WIDE)
        value = from_above + norm_backward(grad_out, unit, factor, gains[0, 2:3, :])
        back[block, :] = value
        back_low[block, :] = value.astype(LOW)
        parts = (grad_out * unit, grad_out, value, from_above)
        return tuple(old + fold(part) for old, part in zip(sums, parts))

    zero = jnp.zeros((8, model), WIDE)
    sums = lax.fori_loop(0, rows // BLOCK, second_norm, (zero,) * 4)

    def shared_sum(row, value):
        row_sum = jnp.sum(value, axis=0, keepdims=True)
        for t in range(tensors):
            rows_eight[t, row : row + 1, :] = row_sum

    for at, value in enumerate(sums):
        shared_sum(at + 2, value)
    keep_back = pltpu.make_async_copy(back_low, back_low_out, out_sem.at[2])
    keep_back.start()
    if linked:
        shared.pass_on(1)
    for copy in loads[1:]:
        copy.wait()
    total[...] = jnp.zeros_like(total)
    for slot in range(2):
        keep_hidden(slot).wait()
        keep_down(slot).wait()

    def keep_qkv(t):
        slot = rem(t, 2)
        return pltpu.make_async_copy(qkv_back.at[slot], qkv_back_out.at[t], out_sem.at[slot])

    @pl.loop(0, tensors)
    def _(t):
        slot = rem(t, 2)

        @pl.when(t > 1)
        def _():
            keep_qkv(t - 2).wait()

        out = mixed[t, :, :, :, 3 * width :].reshape(model, width)
        attended_back[...] = dot(back_low[...], out).astype(LOW)

        def attend_back(image, turn):
            spot = pl.ds(pl.multiple_of(image * padded, padded), padded)
            turn[0] = flip(qkv[t, spot, width : 2 * width], unit)
            for head in range(heads):
                lanes = head * HEAD
                query = qkv[t, spot, lanes : lanes + HEAD]
                value = qkv[t, spot, 2 * width + lanes : 2 * width + lanes + HEAD]
                grad = attended_back[spot, lanes : lanes + HEAD]
                prob_low = probs[t, image, head]
                prob = prob_low.astype(WIDE)
                weighted = prob * dot(value, grad, 1, 1)
                score_back = weighted - prob * jnp.sum(weighted, axis=0, keepdims=True)
                score_back = (score_back * scale).astype(LOW)
                query_back = dot(turn[0, lanes : lanes + HEAD, :], score_back)
                turn[1, lanes : lanes + HEAD, :] = query_back.astype(LOW)
                begin = width + lanes
                qkv_back[slot, spot, begin : begin + HEAD] = dot(score_back, query).astype(LOW)
                begin = 2 * width + lanes
                qkv_back[slot, spot, begin : begin + HEAD] = dot(prob_low, grad).astype(LOW)

            qkv_back[slot, spot, :width] = flip(turn[1], unit)

        @pl.loop(0, images // 2)
        def _(pair):
            for at in range(2):
                attend_back(2 * pair + at, turn.at[at])

        keep_qkv(t).start()
        bias_rows[t] = jnp.sum(qkv_back[slot].astype(WIDE), axis=0, keepdims=True)
        wide = mixed[t, :, :, :, : 3 * width].reshape(model, 3 * width)
        total[...] += dot(qkv_back[slot], wide, 1, 1)
    def first_norm(at, sums):
        block = block_at(at)
        unit, factor = norm_parts(tokens[block, :].astype(WIDE))
        grad_out = total[block, :]
        back[block, :] += norm_backward(grad_out, unit, factor, gains[0, 0:1, :])
        parts = (grad_out * unit, grad_out)
        return tuple(old + fold(part) for old, part in zip(sums, parts))

    sums = lax.fori_loop(0, rows // BLOCK, first_norm, (zero,) * 2)
    for at, value in enumerate(sums):
        shared_sum(at, value)
    pack_images(back, work, images, padded)
    packed_grad[...] = work[: packed_grad.shape[0], :].astype(LOW)

    vec_grads[...] = jnp.zeros_like(vec_grads)

    @pl.loop(0, tensors)
    def _(t):
        for place in range(places):
            vec_grads[t, place, :, :slab] = rows_eight[t, :, place * slab : (place + 1) * slab]
            vec_grads[t, place, 6:7, :part] = bias_rows[t, :, place * part : (place + 1) * part]
            begin = 2 * width + place * part
            vec_grads[t, place, 6:7, part : 2 * part] = bias_rows[t, :, begin : begin + part]

    keep_back.wait()
    for slot in range(2):
        keep_qkv(slot).wait()
    if linked:
        shared.finish()


def chain(packed, tokens, cotangent, cot_t, gains, weights, qkv, probs, middle, slope, hidden, places, linked):
    rows, model = tokens.shape
    tensors, hidden_width = weights.shape[1], weights.shape[-1]
    width = hidden_width // 4
    dma = pltpu.SemaphoreType.DMA
    whole = (tensors,) + packed.shape if linked else (8, 128)
    outs = (
        (packed.shape, LOW),
        (whole, LOW),
        ((tensors, rows, hidden_width), LOW),
        ((rows, model), LOW),
        ((tensors, rows, 3 * width), LOW),
        ((tensors, places, 8, 128), WIDE),
        (weights.shape[1:], LOW),
    )
    return pl.pallas_call(
        partial(chain_kernel, linked=linked),
        out_shape=[jax.ShapeDtypeStruct(shape, dtype) for shape, dtype in outs],
        in_specs=[ANY, ANY, VMEM, ANY, VMEM] + [ANY] * 6,
        out_specs=[VMEM] + [ANY] * 4 + [VMEM, ANY],
        scratch_shapes=[
            pltpu.VMEM((rows, model), LOW),
            pltpu.VMEM((model, rows), LOW),
            pltpu.VMEM(weights.shape[1:], LOW),
            pltpu.VMEM((2, 2) + weights.shape[2:], LOW),
            pltpu.VMEM((2, rows, hidden_width), LOW),
            pltpu.VMEM((2, rows, hidden_width), LOW),
            pltpu.VMEM((2,) + weights.shape[2:], LOW),
            pltpu.VMEM(qkv.shape, LOW),
            pltpu.VMEM(probs.shape, LOW),
            pltpu.VMEM((rows, model), WIDE),
            pltpu.VMEM((rows, hidden_width), WIDE),
            pltpu.VMEM((rows, model), WIDE),
            pltpu.VMEM((rows, model), WIDE),
            pltpu.VMEM((rows, model), LOW),
            pltpu.VMEM((2, rows, hidden_width), LOW),
            pltpu.VMEM((rows, width), LOW),
            pltpu.VMEM((2, rows, 3 * width), LOW),
            pltpu.VMEM((tensors, 8, model), WIDE),
            pltpu.VMEM((tensors, 1, 3 * width), WIDE),
            pltpu.VMEM(probs.shape[-2:], LOW),
            pltpu.VMEM((2, 2, width, probs.shape[-1]), LOW),
            dma((6,)),
            dma((2, 4)),
            dma((3,)),
            dma((2,)),
        ]
        + (share_scratch() if linked else []),
        compiler_params=pltpu.CompilerParams(
            vmem_limit_bytes=58 * MEGA, has_side_effects=True, **({"collective_id": 1} if linked else {})
        ),
        name="chain",
    )(packed, tokens, cotangent, cot_t, gains, weights, qkv, probs, middle, slope, hidden)


class Far:
    def __init__(
        self, tokens, weights, gains, biases, out,
        held, window, inputs, normed, qkv, attended, middle, two, work, hidden, packed, mask, unit, turn,
        weight_sem, row_sem, out_sem,
    ):
        self.weights, self.gains, self.biases = weights, gains, biases
        self.held, self.weight_sem = held, weight_sem
        self.inputs, self.normed, self.qkv, self.attended = inputs, normed, qkv, attended
        self.middle, self.two, self.work, self.hidden = middle, two, work, hidden
        self.packed, self.mask, self.unit, self.turn = packed, mask, unit, turn
        self.tensors = weights.shape[1]
        self.rows, self.model = inputs.shape
        self.hidden_width = weights.shape[-1]
        self.width = self.hidden_width // 4
        self.padded = mask.shape[0]
        self.images = self.rows // self.padded
        block = far_block(lax.axis_index("tensor"), self.tensors)
        first = block * (self.images + FAR_SENT) + FAR_SENT
        self.source = Rows(tokens, window, row_sem, first, self.images, self.padded)
        self.store = pltpu.make_async_copy(packed, out, out_sem)

    def weight(self, at):
        group, t = chunk(at)
        slot = rem(at, 2)
        return pltpu.make_async_copy(self.weights.at[group, t], self.held.at[slot], self.weight_sem.at[slot])

    def start(self):
        self.source.fetch()
        self.weight(0).start()
        self.weight(1).start()

    def each_block(self, body):
        @pl.loop(0, self.rows // FAR_STEP)
        def _(at):
            body(pl.ds(pl.multiple_of(at * FAR_STEP, FAR_STEP), FAR_STEP))

    def first_norm(self):
        fill_unit(self.unit)
        fill_mask(self.mask)
        self.source.place(self.inputs)

        def body(block):
            inputs = self.inputs[block, :].astype(WIDE)
            unit, _ = norm_parts(inputs)
            self.normed[block, :] = (unit * self.gains[0, 0:1, :] + self.gains[0, 1:2, :]).astype(LOW)
            self.middle[block, :] = inputs + self.gains[0, 4:5, :]

        self.each_block(body)

    def attention(self, t):
        width = self.width
        slot = rem(t, 2)
        self.weight(t).wait()
        weight = self.held[slot, :, :, :, : 3 * width].reshape(self.model, 3 * width)
        self.qkv[...] = (dot(self.normed[...], weight) + self.biases[t, 6:7, :]).astype(LOW)

        @pl.loop(0, self.images // 2)
        def _(pair):
            for at in range(2):
                attend(2 * pair + at, self.qkv, self.attended, self.mask, self.unit, self.turn.at[at])

        weight = self.held[slot, :, :, :, 3 * width :].reshape(self.model, width)
        self.middle[...] += dot(self.attended[...], weight, 1, 1)
        self.weight(t + 2).start()

    def second_norm(self):
        def body(block):
            values = self.middle[block, :]
            unit, _ = norm_parts(values)
            self.two[block, :] = (unit * self.gains[0, 2:3, :] + self.gains[0, 3:4, :]).astype(LOW)
            self.middle[block, :] = values + self.gains[0, 5:6, :]

        self.each_block(body)

    def up(self, t):
        at = self.tensors + 2 * t
        self.weight(at).wait()
        self.work[...] = dot(self.two[...], self.held[rem(at, 2)].reshape(self.model, self.hidden_width))

        @pl.when(t + 1 < self.tensors)
        def _():
            self.weight(at + 2).start()

        def body(block):
            value = self.work[block, :] + self.gains[t, 7:8, :]
            self.hidden[block, :] = (value * gelu_parts(value)[0]).astype(LOW)

        self.each_block(body)

    def down(self, t):
        at = self.tensors + 2 * t + 1
        self.weight(at).wait()
        weight = self.held[rem(at, 2)].reshape(self.model, self.hidden_width)
        self.middle[...] += dot(self.hidden[...], weight, 1, 1)

        @pl.when(t + 1 < self.tensors)
        def _():
            self.weight(at + 2).start()

    def step(self, n):
        tensors = self.tensors
        begin = tensors + 4

        @pl.when(n == 1)
        def _():
            self.first_norm()

        @pl.when(jnp.logical_and(n > 1, n <= tensors + 1))
        def _():
            self.attention(n - 2)

        @pl.when(n == tensors + 2)
        def _():
            self.second_norm()

        feeding = jnp.logical_and(n >= begin, n < begin + 2 * tensors)

        @pl.when(jnp.logical_and(feeding, rem(n, 2) == 0))
        def _():
            self.up(div(n - begin, 2))
            self.down(div(n - begin, 2))

        @pl.when(n == begin + 2 * tensors - 1)
        def _():
            self.finish()

    def finish(self):
        pack_images(self.middle, self.work, self.images, self.padded)
        self.packed[...] = self.work[: self.packed.shape[0], :].astype(LOW)
        self.store.start()

    def wait(self):
        self.store.wait()


def grads_kernel(
    packed, vec_grads, normed_in, two_in, back_in, qkv_back_in, attended_in, hidden_back_in, down_grads,
    tokens, weights, gains, biases,
    tokens_grad, total_out, vec_out, far_out,
    flat, normed_t, two_t, back_t, acts, mixed_acts, attended_acts, staged,
    pair, x_half, y_half, x_full, y_full, z_sum, vec_pair, vec_x, vec_y, vec_z,
    in_sem, act_sem, keep_sem, vec_send, vec_recv, send, recv, *more,
    linked,
):
    share_sems, far_scratch = more[:3], more[3:]
    tensors, rows, hidden_width = hidden_back_in.shape
    width = hidden_width // 4
    chunks = 3 * tensors
    z = lax.axis_index("tensor")

    def tensor_at(step):
        return z_partner(z, tensors - 1 - step) if linked else step

    def fetch(n, group):
        t, slot = tensor_at(chunk(n)[1]), rem(n, 2)
        pairs = (
            [(qkv_back_in, mixed_acts), (attended_in, attended_acts)],
            [(hidden_back_in, acts)],
            [(down_grads, staged)],
        )[group]
        return [
            pltpu.make_async_copy(src.at[t], dst.at[rem(n, dst.shape[0])], act_sem.at[slot, at])
            for at, (src, dst) in enumerate(pairs)
        ]

    def start(copies):
        for copy in copies:
            copy.start()

    pairs = ((normed_in, normed_t), (back_in, back_t), (two_in, two_t))
    loads = [pltpu.make_async_copy(src, flat.at[at], in_sem.at[at]) for at, (src, _) in enumerate(pairs)]
    start(loads)
    start(fetch(0, 0))

    if linked:
        chip, core, _, x_chip, y_chip, far_chip = position()
        x_dev, y_dev, other = (x_chip * 2 + core, z), (y_chip * 2 + core, z), (chip * 2 + 1 - core, z)
        half = pair.shape[2] // 2
        greet()
        shared = Share(packed, tokens_grad, *share_sems)
        shared.start()
        far = Far(tokens, weights, gains, biases, far_out, *far_scratch)
        far.start()

        def link(n, kind):
            sems = (send.at[n, kind], recv.at[n, kind])
            if kind == 0:
                return remote(staged.at[rem(n, 4), :, 1 - core], pair.at[n], *sems, other)
            if kind == 1:
                return remote(pair.at[n, far_chip, pl.ds(0, half)], x_half.at[n], *sems, x_dev)
            if kind == 2:
                return remote(pair.at[n, far_chip, pl.ds(half, half)], y_half.at[n], *sems, y_dev)
            if kind == 3:
                return remote(pair.at[n, x_chip], x_full.at[n], *sems, x_dev)
            return remote(pair.at[n, y_chip], y_full.at[n], *sems, y_dev)

        inner = rem(z, 2) + div(z, 2) == 1

        def z_link(n, kind):
            step = chunk(n)[1]
            step_there = step + 1 - 2 * rem(step, 2) if kind == 5 else tensors - 1 - step
            there = n + (step_there - step) * (1 + div(n + 4, 8))
            to = (chip * 2 + core, z_partner(z, 1 if kind == 5 else 3))
            return remote(
                pair.at[n, chip], z_sum.at[kind - 5, there], send.at[n, kind], recv.at[there, kind], to
            )

        def z_wait(n, kind):
            spot = z_sum.at[kind - 5, n]
            remote(spot, spot, send.at[n, kind], recv.at[n, kind], other).wait_recv()

        def add(ref, value):
            ref[...] = ref[...] + value

        def first(n):
            link(n, 0).wait_recv()
            link(n, 0).wait_send()
            slot = rem(n, 4)
            add(pair.at[n, far_chip], staged[slot, far_chip, core])
            link(n, 1).start()
            link(n, 2).start()
            for where in (x_chip, y_chip, chip):
                add(pair.at[n, where], staged[slot, where, core])

        def second(n):
            link(n, 1).wait_recv()
            add(pair.at[n, y_chip, pl.ds(0, half)], x_half[n])
            link(n, 4).start()
            link(n, 2).wait_recv()
            add(pair.at[n, x_chip, pl.ds(half, half)], y_half[n])
            link(n, 3).start()

        def third(n):
            link(n, 3).wait_recv()
            link(n, 4).wait_recv()
            mine = pair.at[n, chip]
            total = mine[...].astype(WIDE) + x_full[n].astype(WIDE) + y_full[n].astype(WIDE)
            mine[...] = total.astype(LOW)

            @pl.when(jnp.logical_and(chunk(n)[1] < tensors - 1, jnp.logical_not(inner)))
            def _():
                z_link(n, 5).start()

        def fourth(n):
            step = chunk(n)[1]

            @pl.when(jnp.logical_and(inner, step < 2))
            def _():
                z_wait(n, 5)
                add(pair.at[n, chip], z_sum[0, n])
                z_link(n, 6).start()

            @pl.when(jnp.logical_and(inner, step == 2))
            def _():
                z_wait(n, 6)
                add(pair.at[n, chip], z_sum[1, n])
                z_link(n, 5).start()

        def vec_link(step, kind):
            sems = (vec_send.at[step, kind], vec_recv.at[step, kind])
            t = z_partner(z, step)
            if kind == 0:
                return remote(vec_grads.at[t, :, 1 - core], vec_pair.at[step], *sems, other)
            if kind == 1:
                return remote(vec_pair.at[step, far_chip], vec_x.at[0, step], *sems, x_dev)
            if kind == 3:
                return remote(vec_pair.at[step, x_chip], vec_x.at[1, step], *sems, x_dev)
            if kind == 4:
                return remote(vec_pair.at[step, y_chip], vec_y.at[step], *sems, y_dev)
            return remote(vec_pair.at[step, chip], vec_z.at[step], *sems, (chip * 2 + core, t))

        steps = range(4)
        for step in steps:
            vec_link(step, 0).start()

        def vec_stage(stage):
            for step in steps:
                if stage == 0:
                    vec_link(step, 0).wait_recv()
                    vec_pair[step] += vec_grads[z_partner(z, step), :, core]
                    vec_link(step, 1).start()
                if stage == 1:
                    vec_link(step, 1).wait_recv()
                    add(vec_pair.at[step, y_chip], vec_x[0, step])
                    vec_link(step, 4).start()
                    vec_link(step, 3).start()
                if stage == 2:
                    vec_link(step, 3).wait_recv()
                    vec_link(step, 4).wait_recv()
                    add(vec_pair.at[step, chip], vec_x[1, step] + vec_y[step])
                    if step:
                        vec_link(step, 5).start()
                if stage == 3 and step:
                    vec_link(step, 5).wait_recv()
            if stage == 3:
                mine = vec_pair.at[0, chip]
                vec_out[...] = mine[...] + vec_z[1] + vec_z[2] + vec_z[3]
                for step in steps:
                    for kind in (0, 1, 3, 4, 5):
                        if kind < 5 or step:
                            vec_link(step, kind).wait_send()

    for load, (_, dst), at in zip(loads, pairs, range(3)):
        load.wait()
        dst[...] = flat[at].T
        if linked:
            vec_stage(at)

    def keep(n):
        group, step = chunk(n)
        return pltpu.make_async_copy(staged.at[rem(n, 4)], total_out.at[group, step], keep_sem.at[rem(n, 2)])

    def clear(n):
        if not linked:

            @pl.when(n > 1)
            def _():
                keep(n - 2).wait()

    shape = staged.shape[1:-1]

    @pl.loop(0, chunks + 6 if linked else chunks)
    def _(n):
        slot, place = rem(n, 2), rem(n, 4)
        paired = jnp.logical_and(n >= tensors, n < chunks)
        clear(n)

        @pl.when(n < tensors)
        def _():
            @pl.when(n + 1 < tensors)
            def _():
                start(fetch(n + 1, 0))

            @pl.when(n + 1 == tensors)
            def _():
                start(fetch(n + 1, 1))

            for copy in fetch(n, 0):
                copy.wait()
            wide = dot(normed_t[...], mixed_acts[slot]).astype(LOW)
            staged[place, :, :, :, : 3 * width] = wide.reshape(shape + (3 * width,))
            out = dot(back_t[...], attended_acts[slot]).astype(LOW)
            staged[place, :, :, :, 3 * width :] = out.reshape(shape + (width,))

        @pl.when(jnp.logical_and(paired, slot == 0))
        def _():
            start(fetch(n + 1, 2))
            for copy in fetch(n, 1):
                copy.wait()
            staged[place] = dot(two_t[...], acts[slot]).astype(LOW).reshape(shape + (hidden_width,))

        @pl.when(jnp.logical_and(paired, slot == 1))
        def _():
            @pl.when(n + 1 < chunks)
            def _():
                start(fetch(n + 1, 1))

            for copy in fetch(n, 2):
                copy.wait()

        if not linked:
            keep(n).start()
            return

        @pl.when(n < chunks)
        def _():
            link(n, 0).start()

        far.step(n)
        for stage, lag in ((first, 1), (second, 2), (third, 3), (fourth, 6)):

            @pl.when(jnp.logical_and(n >= lag, n < chunks + lag))
            def _():
                stage(n - lag)

        for stage, step in enumerate((1, 3, 5, 7)):

            @pl.when(n == step)
            def _():
                shared.pass_on(stage)

    if linked:
        vec_stage(3)
        for group in range(3):
            n = max(n for n in range(chunks) if chunk(n)[0] == group)
            z_wait(n, 5)
            total_out[group] = pair[n, chip].astype(WIDE) + z_sum[0, n].astype(WIDE)

            @pl.when(inner)
            def _():
                z_wait(n, 6)
                total_out[group] += z_sum[1, n].astype(WIDE)

        @pl.loop(0, chunks)
        def _(n):
            for kind in range(1, 5):
                link(n, kind).wait_send()
            step = chunk(n)[1]

            @pl.when(jnp.logical_or(jnp.logical_and(step < tensors - 1, jnp.logical_not(inner)), jnp.logical_and(step == 2, inner)))
            def _():
                z_link(n, 5).wait_send()

            @pl.when(jnp.logical_and(step < 2, inner))
            def _():
                z_link(n, 6).wait_send()

        far.wait()
        shared.finish()
    else:
        keep(chunks - 2).wait()
        keep(chunks - 1).wait()


def weight_grads(
    packed, vec_grads, normed, two, back_low, qkv_back, attended, hidden_back, down_grads,
    tokens, weights, gains, biases, places, linked,
):
    tensors, rows, hidden_width = hidden_back.shape
    model = normed.shape[1]
    width = hidden_width // 4
    chunks = 3 * tensors
    dma = pltpu.SemaphoreType.DMA
    if linked:
        slab, chips = model // places, places // 2
        blocks = (chips, 2, slab, hidden_width)
        total = (3, slab, hidden_width), WIDE
        whole = (tensors,) + packed.shape
        vec_out = (8, 128)
        landing = [
            pltpu.VMEM((chunks, chips, slab, hidden_width), LOW),
            pltpu.VMEM((chunks, slab // 2, hidden_width), LOW),
            pltpu.VMEM((chunks, slab // 2, hidden_width), LOW),
            pltpu.VMEM((chunks, slab, hidden_width), LOW),
            pltpu.VMEM((chunks, slab, hidden_width), LOW),
            pltpu.VMEM((2, chunks, slab, hidden_width), LOW),
            pltpu.VMEM((4, chips, 8, 128), WIDE),
            pltpu.VMEM((2, 4, 8, 128), WIDE),
            pltpu.VMEM((4, 8, 128), WIDE),
            pltpu.VMEM((4, 8, 128), WIDE),
        ]
        vec_grads = vec_grads.reshape(tensors, chips, 2, 8, 128)
    else:
        blocks = (1, 1, model, hidden_width)
        total = (3, tensors) + blocks, LOW
        whole = vec_out = (8, 128)
        landing = [pltpu.VMEM((8, 128), WIDE)] * 10
    far_scratch = []
    if linked:
        padded = round_up(SEQ, ROWS)
        images = rows // padded - FAR_SENT
        far_rows, far_packed = images * padded, (round_up(images * SEQ, ROWS), model)
        far_scratch = [
            pltpu.VMEM((2,) + weights.shape[2:], LOW),
            pltpu.VMEM((images, padded + ROWS, model), LOW),
            pltpu.VMEM((far_rows, model), LOW),
            pltpu.VMEM((far_rows, model), LOW),
            pltpu.VMEM((far_rows, 3 * width), LOW),
            pltpu.VMEM((far_rows, width), LOW),
            pltpu.VMEM((far_rows, model), WIDE),
            pltpu.VMEM((far_rows, model), LOW),
            pltpu.VMEM((far_rows, hidden_width), WIDE),
            pltpu.VMEM((far_rows, hidden_width), LOW),
            pltpu.VMEM(far_packed, LOW),
            pltpu.VMEM((padded, padded), WIDE),
            pltpu.VMEM((padded, padded), LOW),
            pltpu.VMEM((images, 2, width, padded), LOW),
            dma((2,)),
            dma((images,)),
            dma,
        ]
    outs = ((whole, LOW), total, (vec_out, WIDE), (far_packed if linked else (8, 128), LOW))
    return pl.pallas_call(
        partial(grads_kernel, linked=linked),
        out_shape=[jax.ShapeDtypeStruct(shape, dtype) for shape, dtype in outs],
        in_specs=[ANY, VMEM] + [ANY] * 9 + [VMEM] * 2,
        out_specs=[ANY, VMEM if linked else ANY, VMEM, ANY],
        scratch_shapes=[pltpu.VMEM((3, rows, model), LOW)]
        + [pltpu.VMEM((model, rows), LOW)] * 3
        + [
            pltpu.VMEM((2, rows, hidden_width), LOW),
            pltpu.VMEM((2, rows, 3 * width), LOW),
            pltpu.VMEM((2, rows, width), LOW),
            pltpu.VMEM((4,) + blocks, LOW),
        ]
        + landing
        + [
            dma((3,)),
            dma((2, 2)),
            dma((2,)),
            dma((4, 6)),
            dma((4, 6)),
            dma((chunks, 7)),
            dma((chunks, 7)),
        ]
        + (share_scratch() if linked else [])
        + far_scratch,
        compiler_params=pltpu.CompilerParams(
            vmem_limit_bytes=58 * MEGA, has_side_effects=True, **({"collective_id": 2} if linked else {})
        ),
        name="weight_grads",
    )(
        packed, vec_grads, normed, two, back_low, qkv_back, attended, hidden_back, down_grads,
        tokens, weights, gains, biases,
    )


def adam_step(weight, gradient, first, second, rate, decay):
    first = BETA_ONE * first + (1.0 - BETA_ONE) * gradient
    second = BETA_TWO * second + (1.0 - BETA_TWO) * gradient * gradient
    corr_one = 1.0 - BETA_ONE**STEP
    corr_two = 1.0 - BETA_TWO**STEP
    updated = weight * (1.0 - rate * decay) - rate * (first / corr_one) / (
        jnp.sqrt(second / corr_two) + EPS_ADAM
    )
    return (first, second, updated)


def finish_kernel(*refs, linked, tensors, rows, slab, groups):
    refs = list(refs)
    wholes = [refs.pop(0) for _ in range(3)] if linked else []
    total, vec = refs.pop(0), refs.pop(0)
    inputs = [refs.pop(0) for _ in range(18)]
    flats = [refs.pop(0) for _ in range(2)] if linked else []
    outputs = [refs.pop(0) for _ in range(18)]
    held = [refs.pop(0) for _ in range(18)]
    news = [refs.pop(0) for _ in range(18)]
    small_in, small_out = refs.pop(0), refs.pop(0)
    params, moments = held[:6], held[6:]
    fetches = [pltpu.make_async_copy(inputs[at], held[at], small_in.at[at]) for at in range(18)]
    if linked:
        landed, far_landed, done, in_sem, out_sem, far_sem = refs

        far = far_block(lax.axis_index("tensor"), tensors)

        sent, far_rows = FAR_SENT * SEQ, rows - FAR_SENT * SEQ
        far_load = pltpu.make_async_copy(wholes[2], far_landed, far_sem)

        def load(at, t):
            return pltpu.make_async_copy(wholes[at].at[t], landed.at[at, t], in_sem.at[at, t])

        def store(at, t):
            begin, end = t * rows // ROWS * ROWS, (t + 1) * rows // ROWS * ROWS
            if t == tensors - 1:
                end = tensors * rows
            spot = pl.ds(begin, end - begin)
            return pltpu.make_async_copy(done.at[at, spot], flats[at].at[spot], out_sem.at[at, t])

        parts = [(at, t) for at in range(2) for t in range(tensors)]
        far_load.start()
        for part in parts:
            load(*part).start()
        for copy in fetches:
            copy.start()
        far_load.wait()
        for at, t in parts:
            load(at, t).wait()
            done[at, t * rows : (t + 1) * rows, :] = landed[at, t, :rows, :]
            if at == 0 and t in (0, tensors - 1):

                @pl.when(far == t)
                def _():
                    done[at, t * rows + sent : (t + 1) * rows, :] = far_landed[:far_rows, :]

            store(at, t).start()

    else:
        for copy in fetches:
            copy.start()

    width = total.shape[2] // 4

    for copy in fetches:
        copy.wait()

    def step(at, gradient, rate, decay, pick=()):
        weight, first, second = params[at], moments[2 * at], moments[2 * at + 1]
        values = adam_step(weight[pick], gradient, first[pick], second[pick], rate, decay)
        for out, value in zip(news[3 * at : 3 * at + 3], values):
            out[pick] = value

    for at in range(3):
        step(0, total[0, :, at * width : (at + 1) * width], RATE_MATRIX, DECAY_MATRIX, (at,))
    every = (slice(None),)
    step(1, total[0, :, 3 * width :].T, RATE_MATRIX, DECAY_MATRIX, every)
    step(2, total[1], RATE_MATRIX, DECAY_MATRIX, every)
    step(3, total[2], RATE_MATRIX, DECAY_MATRIX, every)
    step(4, vec[:6, :slab], RATE_VECTOR, 0.0, every)
    columns = vec[...].T
    shape = (columns.shape[0], 6 * groups)
    lane, row = (lax.broadcasted_iota(jnp.int32, shape, dim) for dim in (1, 0))
    attention = jnp.where(row < groups, 6 * row, jnp.where(row < 2 * groups, 6 * (row - groups) + 1, -1))
    hidden = jnp.where(row < 4 * groups, 6 * div(row, 4) + 2 + rem(row, 4), -1)
    picked = jnp.where(lane == attention, columns[:, 6:7], 0.0) + jnp.where(
        lane == hidden, columns[:, 7:8], 0.0
    )
    step(5, jnp.sum(picked, axis=0, keepdims=True), RATE_VECTOR, 0.0, every)
    stores = [pltpu.make_async_copy(news[at], outputs[at], small_out.at[at]) for at in range(18)]
    for copy in stores:
        copy.start()
    if linked:
        for part in parts:
            store(*part).wait()
    for copy in stores:
        copy.wait()


def finish(wholes, total, vec, params, moments, tensors, rows, slab, groups, linked):
    small = params + moments
    scratch = [pltpu.VMEM(value.shape, WIDE) for value in small]
    scratch += [pltpu.VMEM(param.shape, WIDE) for param in params for _ in range(3)]
    scratch += [pltpu.SemaphoreType.DMA((18,))] * 2
    outs, passed = [], ()
    if linked:
        passed = wholes
        model = wholes[0].shape[2]
        scratch += [
            pltpu.VMEM((2,) + wholes[0].shape, LOW),
            pltpu.VMEM(wholes[2].shape, LOW),
            pltpu.VMEM((2, tensors * rows, model), LOW),
            pltpu.SemaphoreType.DMA((2, tensors)),
            pltpu.SemaphoreType.DMA((2, tensors)),
            pltpu.SemaphoreType.DMA,
        ]
        outs = [jax.ShapeDtypeStruct((tensors * rows, model), LOW)] * 2
    news = [jax.ShapeDtypeStruct(param.shape, WIDE) for param in params for _ in range(3)]
    results = pl.pallas_call(
        partial(finish_kernel, linked=linked, tensors=tensors, rows=rows, slab=slab, groups=groups),
        out_shape=outs + news,
        in_specs=[ANY] * len(passed) + [VMEM] * 2 + [ANY] * 18,
        out_specs=[ANY] * (len(outs) + 18),
        scratch_shapes=scratch,
        compiler_params=pltpu.CompilerParams(vmem_limit_bytes=58 * MEGA),
        name="finish",
    )(*passed, total, vec, *small)
    if linked:
        return results[:2], list(results[2:])
    return wholes, list(results)


def own_parts(params, slab, width):
    qkv, out, up, down_t, shared, split = params
    mixed = jnp.concatenate([qkv[0], qkv[1], qkv[2], out.T], axis=1)
    table = split.reshape(-1, 6)
    rows = [shared, jnp.concatenate([table[:, 0], table[:, 1]])[None], table[:, 2:].reshape(1, -1)]
    vec = jnp.concatenate([jnp.pad(row, ((0, 0), (0, 128 - row.shape[1]))) for row in rows])
    return jnp.stack([mixed, up, down_t]).astype(LOW), vec


def per_device(
    tokens,
    cotangent,
    qkv_weight,
    out_weight,
    up_weight,
    down_weight,
    shared_vectors,
    split_vectors,
    qkv_first,
    qkv_second,
    out_first,
    out_second,
    up_first,
    up_second,
    down_first,
    down_second,
    shared_first,
    shared_second,
    split_first,
    split_second,
    *,
    places,
    tensors,
):
    linked = places == 8 and tensors == 4
    slab, width = qkv_weight.shape[1], qkv_weight.shape[2]
    model = slab * places
    groups = width // places
    rows = tokens.shape[0] // tensors
    images = rows // SEQ

    params = (qkv_weight, out_weight, up_weight, down_weight.T, shared_vectors, split_vectors)
    moments = (
        qkv_first, qkv_second, out_first, out_second, up_first, up_second,
        down_first.T, down_second.T, shared_first, shared_second, split_first, split_second,
    )
    sources = params
    if not linked:
        shard, vec = own_parts(params, slab, width)
        shard = lax.all_gather(lax.all_gather(shard, "dp", axis=1, tiled=True), "tensor", axis=1)
        vec = lax.all_gather(lax.all_gather(vec, "dp"), "tensor")
        sources = (shard, vec.reshape(tensors, places // 2, 2, 8, 128))
    packed, weights, own, back, back_t, gains, biases, *kept = forward(
        tokens, cotangent, sources, images, width, tensors, places, linked
    )
    normed, qkv, probs, attended, middle, two, hidden, slope = kept
    if not linked:
        weights = shard.reshape(3, tensors, 1, 1, model, 4 * width)
    packed_grad, block_out, hidden_back, back_low, qkv_back, vec_grads, down_grads = chain(
        packed, own, back, back_t, gains, weights, qkv, probs, middle, slope, hidden, places, linked
    )
    tokens_grad, total, vec_total, far = weight_grads(
        packed_grad, vec_grads, normed, two, back_low, qkv_back, attended, hidden_back, down_grads,
        tokens, weights, gains, biases, places, linked,
    )
    if linked:
        shares = (block_out, tokens_grad, far)
    else:
        shares = [lax.all_gather(part[:rows], "tensor", axis=0, tiled=True) for part in (packed, packed_grad)]
        total = total.reshape(3, tensors, model, 4 * width)
        total = lax.psum_scatter(total, "dp", scatter_dimension=2, tiled=True)
        total = lax.psum_scatter(total, "tensor", scatter_dimension=1).astype(WIDE)
        vec_total = lax.psum_scatter(vec_grads, "dp", scatter_dimension=1)
        vec_total = lax.psum_scatter(vec_total, "tensor", scatter_dimension=0)
    shares, news = finish(shares, total, vec_total, params, moments, tensors, rows, slab, groups, linked)
    news[9:12] = [new.T for new in news[9:12]]
    return (*shares, *news)


def solution(mesh):
    qkv, rows, cols = P(None, "dp", "tensor"), P("tensor", "dp"), P("dp", "tensor")
    shared, images = P(None, "dp"), P("dp", None)
    params = (qkv, rows, cols, rows, shared, rows)
    moments = tuple(spec for spec in params for _ in range(2))
    results = tuple(spec for spec in params for _ in range(3))
    return jax.shard_map(
        partial(per_device, places=mesh.shape["dp"], tensors=mesh.shape["tensor"]),
        mesh=mesh,
        in_specs=(images, images) + params + moments,
        out_specs=(images, images) + results,
        check_vma=False,
    )
```
